128 devices in a mesh: ctx: 64 (over x, y, z_hi, core), kv: 2 (over z_lo).
Axes of the slice: x: 4, y: 4, z: 4 (z_hi: 2, z_lo: 2; z = z_hi * 2 + z_lo), core: 2. Of those that a mesh axis runs over, the one named last changes fastest.
Arguments:
- query_rows: bfloat16 [8192, 16, 128], P('ctx', 'kv'), may hold values from -5.5 to 5.5
- key_rows: bfloat16 [8192, 2, 128], P('ctx', 'kv'), may hold values from -5.5 to 5.5
- value_rows: bfloat16 [8192, 2, 128], P('ctx', 'kv'), may hold values from -6 to 6
- attn_out: bfloat16 [8192, 16, 128], P('ctx', 'kv'), may hold values from -4 to 4
- attn_grad: bfloat16 [8192, 16, 128], P('ctx', 'kv'), may hold values from -6 to 6
- log_total: float32 [8192, 16], P('ctx', 'kv'), may hold values from -400 to 400, as said below
- stretch_order: int32 [128], replicated, may hold values from 0 to 127, as said below
- moe_rows: bfloat16 [8192, 2048], P(('ctx', 'kv')), may hold values from -6 to 6
- moe_grad: bfloat16 [8192, 2048], P(('ctx', 'kv')), may hold values from -3 to 3
- expert_ids: int32 [8192, 8], P(('ctx', 'kv')), may hold values from 0 to 127, all different within a row; in each aligned block of 64 rows (0 to 63, 64 to 127, ...) at most 5 rows name the same one
- gate_prob: bfloat16 [8192, 8], P(('ctx', 'kv')), may hold values from 0.049804688 to 0.29882812
- gate_weight: bfloat16 [128, 2048, 768], P(('ctx', 'kv')), may hold values from -0.125 to 0.125
- up_weight: bfloat16 [128, 2048, 768], P(('ctx', 'kv')), may hold values from -0.125 to 0.125
- down_weight: bfloat16 [128, 768, 2048], P(('ctx', 'kv')), may hold values from -0.21875 to 0.21875
Outputs:
- d_query: bfloat16 [8192, 16, 128], P('ctx', 'kv')
- d_key: bfloat16 [8192, 2, 128], P('ctx', 'kv')
- d_value: bfloat16 [8192, 2, 128], P('ctx', 'kv')
- d_rows: bfloat16 [8192, 2048], P(('ctx', 'kv'))
- d_gates: bfloat16 [8192, 8], P(('ctx', 'kv'))
- grad_gate: bfloat16 [128, 2048, 768], P(('ctx', 'kv'))
- grad_up: bfloat16 [128, 2048, 768], P(('ctx', 'kv'))
- grad_down: bfloat16 [128, 768, 2048], P(('ctx', 'kv'))
The draws below stay inside these ranges and needn't reach their ends.
Inputs may be any that keep to these rules, and one draw needn't show every extreme that they name: `stretch_order`: entries 2 d and 2 d + 1 are the stretches stored by context index d: a stretch c below 64 and 127 - c; every stretch appears once. `expert_ids`: each row names 8 different experts. Among the 64 rows of one device no expert is named more than 5 times, a bound that some block reaches. `log_total`: the log of the sum of exp(scores) over the allowed keys of the row, from the forward pass.
All inputs are finite; a program needn't handle non-finite values.
Results may differ from the reference program's by a relative error of at most 0.013.
Values may be sent and summed in bfloat16 or wider, within the bound.
A program may use at most 128 MiB of HBM per device.

```python
import math
import jax
import jax.numpy as jnp
import numpy as np
from jax import lax

D = 2048
FF = 768
HEAD = 128
GROUP = 8
TOP = 8
KVHEADS = 2
QHEADS = 16
EXPERTS = 128
SEQ = 8192
STRETCH = 64
STRETCHES = 128
ROWS_DEV = 64
CAP = 5
N_CTX = 64
N_KV = 2


def draw_query_rows(key, part):
    key = jax.random.fold_in(key, 2)
    drawn = jnp.clip(jax.random.normal(key, (SEQ, QHEADS, HEAD), jnp.float32), -5.5, 5.5)
    return drawn.astype(jnp.bfloat16)


def draw_key_rows(key, part):
    key = jax.random.fold_in(key, 1)
    drawn = jnp.clip(jax.random.normal(key, (SEQ, KVHEADS, HEAD), jnp.float32), -5.5, 5.5)
    return drawn.astype(jnp.bfloat16)


def draw_stretch_order(key, part):
    key = jax.random.fold_in(key, 3)
    early = jax.random.permutation(key, STRETCHES // 2).astype(jnp.int32)
    return jnp.stack([early, STRETCHES - 1 - early], axis=1).reshape(-1).astype(jnp.int32)


def draw_log_total(key, part):
    queries = draw_query_rows(key, part).astype(jnp.float32).reshape(SEQ, KVHEADS, GROUP, HEAD)
    keys_all = draw_key_rows(key, part).astype(jnp.float32)
    order = draw_stretch_order(key, part)
    row_ids = jnp.arange(SEQ, dtype=jnp.int32)
    positions = order[row_ids // STRETCH] * STRETCH + row_ids % STRETCH
    block_rows = math.gcd(SEQ, 256)
    score_scale = 1.0 / math.sqrt(HEAD)

    def one_block(block_index):
        first_row = block_index * block_rows
        block_q = lax.dynamic_slice_in_dim(queries, first_row, block_rows, 0)
        query_pos = lax.dynamic_slice_in_dim(positions, first_row, block_rows, 0)
        allowed = (positions[None, :] <= query_pos[:, None])[:, None, None, :]
        scores = jnp.einsum('qgid,kgd->qgik', block_q, keys_all) * score_scale
        masked = jnp.where(allowed, scores, -1e+30)
        top_score = jnp.max(masked, axis=3, keepdims=True)
        total = jnp.sum(jnp.where(allowed, jnp.exp(masked - top_score), 0.0), axis=3, keepdims=True)
        return (top_score + jnp.log(total))[..., 0].reshape(block_rows, QHEADS)
    blocks = lax.map(one_block, jnp.arange(SEQ // block_rows, dtype=jnp.int32))
    return blocks.reshape(SEQ, QHEADS).astype(jnp.float32)


def block_levels(key, shape, shards, smallest, top_value):
    level, own = 1.0, jax.random.fold_in(key, 6)
    for axis_at, parts in shards:
        draws = jnp.exp(jax.random.uniform(jax.random.fold_in(own, axis_at), (parts,), jnp.float32, smallest / len(shards), top_value / len(shards)))
        level = level * jnp.repeat(draws, shape[axis_at] // parts).reshape([-1 if axis == axis_at else 1 for axis in range(len(shape))])
    return level


def assign_block(own_key, own, number, rows, amount, top, reach, skew):
    sequence = jax.random.permutation(own_key, amount)
    heavy_load, usual = portions_of(amount, rows * top, reach, skew, True), portions_of(amount, rows * top, reach, skew, False)
    places = jnp.arange(amount)

    def named(sizes, rotation):
        used = int((sizes > 0).sum())
        fixed = max(1, used // 4)
        shifted = fixed + (places - fixed + rotation * (used - fixed)) % max(1, amount - fixed)
        return jnp.zeros((amount,), jnp.int32).at[sequence[jnp.where(places < fixed, places, shifted)]].set(jnp.asarray(sizes, jnp.int32))

    sizes = jnp.where(number % 4 == 0, named(heavy_load, number // 4), named(usual, number - number // 4 - 1))
    mixed = jax.random.permutation(jax.random.fold_in(own, 3), amount)
    giver, receiver = mixed[0:amount // 2 * 2:2], mixed[1:amount // 2 * 2:2]
    room = jnp.minimum(sizes[giver] - 1, reach - sizes[receiver]) // 2
    room = jnp.where((giver == sequence[0]) | (receiver == sequence[0]) | (sizes[receiver] == 0), 0, jnp.maximum(room, 0))
    shifted = jax.random.randint(jax.random.fold_in(own, 4), (amount // 2,), 0, 1 << 20) % (room + 1)
    sizes = sizes.at[giver].add(-shifted).at[receiver].add(shifted)
    labels = jnp.searchsorted(jnp.cumsum(sizes), jnp.arange(rows * top), side="right").astype(jnp.int32)
    listing = labels.reshape(top, rows).T
    listing = listing[jax.random.permutation(jax.random.fold_in(own, 1), rows)]
    rotation = jax.random.randint(jax.random.fold_in(own, 2), (rows, 1), 0, top)
    return jnp.take_along_axis(listing, (jnp.arange(top)[None, :] + rotation) % top, axis=1)


def portions_of(amount, total, most, slope, full):
    loads = [(1 << 20) // math.isqrt(standing ** slope) + 1 for standing in range(1, amount + 1)]
    largest = most if full else min(most, max(-(-total // amount), total * loads[0] // sum(loads)))
    least = 1 if total - largest >= amount - 1 else 0
    counts, rest = [largest] + [least] * (amount - 1), total - largest - least * (amount - 1)
    while rest > 0:
        movable = [i for i in range(1, amount) if counts[i] < largest] or [i for i in range(1, amount) if counts[i] < most]
        whole, budget = sum([loads[i] for i in movable]), rest
        for i in movable:
            extra = min(most - counts[i], max(1, budget * loads[i] // whole), rest)
            counts[i] = counts[i] + extra
            rest = rest - extra
    return np.array(counts)


def normal_values(rng, extent, deviation, most, cuts=(), kind=jnp.bfloat16):
    level = block_levels(rng, extent, cuts, -0.22, 0.18) if cuts else 1.0
    values = jax.random.normal(rng, extent, jnp.float32) * deviation * level
    return jnp.minimum(jnp.maximum(values, -most), most).astype(kind)


def setup_inputs(seed: int = 0) -> dict:
    streams_of = jax.random.split(jax.random.key(seed), 15)
    query_rows = draw_query_rows(jax.random.fold_in(streams_of[14], 71), 0)
    key_rows = draw_key_rows(jax.random.fold_in(streams_of[14], 71), 0)
    value_rows = normal_values(streams_of[2], (SEQ, KVHEADS, HEAD), 1.0, 6.0, ((0, 64), (1, 2)))
    attn_out = normal_values(streams_of[3], (SEQ, QHEADS, HEAD), 0.3, 4.0, ((0, 64), (1, 2)))
    attn_grad = normal_values(streams_of[4], (SEQ, QHEADS, HEAD), 1.0, 6.0, ((0, 64), (1, 2)))
    log_total = draw_log_total(jax.random.fold_in(streams_of[14], 71), 0)
    stretch_order = draw_stretch_order(jax.random.fold_in(streams_of[14], 71), 0)
    moe_rows = normal_values(streams_of[7], (SEQ, D), 1.0, 6.0, ((0, 128),))
    moe_grad = normal_values(streams_of[8], (SEQ, D), 0.2, 3.0, ((0, 128),))
    expert_ids_keys = jax.random.split(jax.random.fold_in(streams_of[9], 1), SEQ // ROWS_DEV)
    expert_ids_turns = jax.random.permutation(jax.random.fold_in(streams_of[9], 3), SEQ // ROWS_DEV)
    expert_ids = jax.vmap(lambda own, number: assign_block(jax.random.fold_in(streams_of[9], 2), own, number, ROWS_DEV, EXPERTS, TOP, CAP, 2))(expert_ids_keys, expert_ids_turns).reshape((SEQ, TOP))
    gate_prob = jnp.clip(0.049804688 + 0.24902344 * jax.random.uniform(streams_of[10], (SEQ, TOP), jnp.float32) ** block_levels(streams_of[10], (SEQ, TOP), ((0, 128),), -0.2, 0.2), 0.049804688, 0.29882812).astype(jnp.bfloat16)
    gate_weight = normal_values(streams_of[11], (EXPERTS, D, FF), D ** -0.5, 0.125, ((0, 128),))
    up_weight = normal_values(streams_of[12], (EXPERTS, D, FF), D ** -0.5, 0.125, ((0, 128),))
    down_weight = normal_values(streams_of[13], (EXPERTS, FF, D), FF ** -0.5, 0.21875, ((0, 128),))
    return dict(query_rows=query_rows, key_rows=key_rows, value_rows=value_rows, attn_out=attn_out, attn_grad=attn_grad, log_total=log_total, stretch_order=stretch_order, moe_rows=moe_rows, moe_grad=moe_grad, expert_ids=expert_ids, gate_prob=gate_prob, gate_weight=gate_weight, up_weight=up_weight, down_weight=down_weight)


def settle(values):
    return lax.optimization_barrier(values.astype(jnp.bfloat16)).astype(jnp.float32)

def attention_grads(query_rows, key_rows, value_rows, attn_out, attn_grad, log_total, stretch_order):
    score_scale = 1.0 / math.sqrt(HEAD)
    row_ids = jnp.arange(SEQ, dtype=jnp.int32)
    positions = stretch_order[row_ids // STRETCH] * STRETCH + row_ids % STRETCH
    keys_all = key_rows.astype(jnp.float32)
    values_all = value_rows.astype(jnp.float32)
    block_rows = math.gcd(SEQ, 256)

    def visit(state_in, block_index):
        key_acc, value_acc = state_in
        first_row = block_index * block_rows
        queries = lax.dynamic_slice_in_dim(query_rows, first_row, block_rows, 0).astype(jnp.float32).reshape(block_rows, KVHEADS, GROUP, HEAD)
        grads_out = lax.dynamic_slice_in_dim(attn_grad, first_row, block_rows, 0).astype(jnp.float32).reshape(block_rows, KVHEADS, GROUP, HEAD)
        saved_out = lax.dynamic_slice_in_dim(attn_out, first_row, block_rows, 0).astype(jnp.float32).reshape(block_rows, KVHEADS, GROUP, HEAD)
        saved_log = lax.dynamic_slice_in_dim(log_total, first_row, block_rows, 0).astype(jnp.float32).reshape(block_rows, KVHEADS, GROUP)
        row_log = jnp.transpose(saved_log, (1, 0, 2))[..., None]
        query_pos = lax.dynamic_slice_in_dim(positions, first_row, block_rows, 0)
        allowed = (positions[None, :] <= query_pos[:, None])[None, :, None, :]
        scores = jnp.einsum('qgid,kgd->gqik', queries, keys_all) * score_scale
        attn_probs = jnp.where(allowed, jnp.exp(jnp.where(allowed, scores - row_log, 0.0)), 0.0)
        probs_low = settle(attn_probs)
        deltas = jnp.einsum('qgid,qgid->gqi', grads_out, saved_out)[..., None]
        value_grad = jnp.einsum('gqik,qgid->kgd', probs_low, grads_out)
        prob_grad = jnp.einsum('qgid,kgd->gqik', grads_out, values_all)
        score_grad = settle(attn_probs * (prob_grad - deltas))
        query_grad = jnp.einsum('gqik,kgd->qgid', score_grad, keys_all) * score_scale
        key_grad = jnp.einsum('gqik,qgid->kgd', score_grad, queries) * score_scale
        return ((key_acc + key_grad, value_acc + value_grad), query_grad.reshape(block_rows, QHEADS, HEAD).astype(jnp.bfloat16))
    zeros_kv = jnp.zeros((SEQ, KVHEADS, HEAD), jnp.float32)
    (key_acc, value_acc), query_parts = lax.scan(visit, (zeros_kv, zeros_kv), jnp.arange(SEQ // block_rows, dtype=jnp.int32))
    return (query_parts.reshape(SEQ, QHEADS, HEAD), key_acc.astype(jnp.bfloat16), value_acc.astype(jnp.bfloat16))

def expert_grads(rows_in, grads_in, gates_in, gate_mat, up_mat, down_mat):
    gate_act = jnp.dot(rows_in, gate_mat, preferred_element_type=jnp.float32)
    up_act = jnp.dot(rows_in, up_mat, preferred_element_type=jnp.float32)
    gate_sig = jax.nn.sigmoid(gate_act)
    hidden = (gate_act * gate_sig * up_act).astype(jnp.bfloat16)
    projected = jnp.dot(grads_in, down_mat.T, preferred_element_type=jnp.float32)
    slot_gate = lax.optimization_barrier(jnp.sum(projected * hidden.astype(jnp.float32), axis=1)).astype(jnp.bfloat16)
    gate_col = gates_in[:, None]
    hidden_grad = gate_col * projected
    gate_grad = (hidden_grad * up_act * gate_sig * (1.0 + gate_act * (1.0 - gate_sig))).astype(jnp.bfloat16)
    up_grad = (hidden_grad * gate_act * gate_sig).astype(jnp.bfloat16)
    slot_rows = (jnp.dot(gate_grad, gate_mat.T, preferred_element_type=jnp.float32) + jnp.dot(up_grad, up_mat.T, preferred_element_type=jnp.float32)).astype(jnp.bfloat16)
    scaled_grads = (gate_col * grads_in.astype(jnp.float32)).astype(jnp.bfloat16)
    gate_sum = jnp.dot(rows_in.T, gate_grad, preferred_element_type=jnp.float32)
    up_sum = jnp.dot(rows_in.T, up_grad, preferred_element_type=jnp.float32)
    down_sum = jnp.dot(hidden.T, scaled_grads, preferred_element_type=jnp.float32)
    return (slot_rows, slot_gate, gate_sum, up_sum, down_sum)

def moe_grads(moe_rows, moe_grad, expert_ids, gate_prob, gate_weight, up_weight, down_weight):
    most_rows = N_CTX * N_KV * CAP

    def per_expert(state_in, expert):
        row_acc, gate_acc = state_in
        named_here = expert_ids == expert
        chosen = jnp.any(named_here, axis=1)
        picked = jnp.nonzero(chosen, size=most_rows, fill_value=0)[0].astype(jnp.int32)
        live_rows = (jnp.arange(most_rows, dtype=jnp.int32) < jnp.sum(chosen.astype(jnp.int32))).astype(jnp.float32)
        named_rows = named_here[picked].astype(jnp.float32)
        gates_in = lax.optimization_barrier(jnp.sum(named_rows * gate_prob[picked].astype(jnp.float32), axis=1)) * live_rows
        slot_rows, slot_gate, gate_sum, up_sum, down_sum = expert_grads(moe_rows[picked], moe_grad[picked], gates_in, gate_weight[expert], up_weight[expert], down_weight[expert])
        row_acc = row_acc.at[picked].add(slot_rows.astype(jnp.float32) * live_rows[:, None])
        gate_acc = gate_acc.at[picked].add(named_rows * slot_gate.astype(jnp.float32)[:, None] * live_rows[:, None])
        return ((row_acc, gate_acc), (gate_sum.astype(jnp.bfloat16), up_sum.astype(jnp.bfloat16), down_sum.astype(jnp.bfloat16)))
    start_state = (jnp.zeros((SEQ, D), jnp.float32), jnp.zeros((SEQ, TOP), jnp.float32))
    (row_acc, gate_acc), (grad_gate, grad_up, grad_down) = lax.scan(per_expert, start_state, jnp.arange(EXPERTS, dtype=jnp.int32))
    return (row_acc.astype(jnp.bfloat16), gate_acc.astype(jnp.bfloat16), grad_gate, grad_up, grad_down)

def reference(query_rows, key_rows, value_rows, attn_out, attn_grad, log_total, stretch_order, moe_rows, moe_grad, expert_ids, gate_prob, gate_weight, up_weight, down_weight):
    d_query, d_key, d_value = attention_grads(query_rows, key_rows, value_rows, attn_out, attn_grad, log_total, stretch_order)
    d_rows, d_gates, grad_gate, grad_up, grad_down = moe_grads(moe_rows, moe_grad, expert_ids, gate_prob, gate_weight, up_weight, down_weight)
    return (d_query, d_key, d_value, d_rows, d_gates, grad_gate, grad_up, grad_down)
```

```python
import functools
import math

import jax
import jax.numpy as jnp
from jax import lax
from jax.experimental import pallas as pl
from jax.experimental.pallas import tpu as pltpu
from jax.sharding import PartitionSpec as P

MESH = pl.DeviceIdType.MESH
LOG2E = 1.4426950408889634
F32 = jnp.float32
BF16 = jnp.bfloat16
CAP = 5
TILES = 16
DEVS = 128
CHIPS = 32
HALF = 64


def any_partner(step, c, k):
    s = lax.rem(step * 53, DEVS)
    x = lax.rem(c // 16 + lax.rem(s, 4), 4)
    s = s // 4
    y = lax.rem(lax.rem(c // 4, 4) + lax.rem(s, 4), 4)
    s = s // 4
    zh = lax.rem(lax.rem(c // 2, 2) + lax.rem(s, 2), 2)
    s = s // 2
    kk = lax.rem(k + lax.rem(s, 2), 2)
    core = lax.rem(lax.rem(c, 2) + s // 2, 2)
    return ((x * 4 + y) * 2 + zh) * 2 + core, kk


def chip_partner(step, c):
    x = lax.rem(c // 16 + lax.rem(step, 4), 4)
    s = step // 4
    y = lax.rem(lax.rem(c // 4, 4) + lax.rem(s, 4), 4)
    zh = lax.rem(lax.rem(c // 2, 2) + s // 4, 2)
    return (x * 4 + y) * 2 + zh


def dot(a, b):
    return jnp.dot(a, b, preferred_element_type=F32)


def dot_nt(a, b):
    return lax.dot_general(a, b, (((1,), (1,)), ((), ())), preferred_element_type=F32)


def dot_tn(a, b):
    return lax.dot_general(a, b, (((0,), (0,)), ((), ())), preferred_element_type=F32)


def slot_row(block, r):
    return pl.multiple_of((block // 4) * (CAP * HALF) + r * HALF + lax.rem(block, 4) * 16, 16)


def pack_block(block, perm, flat, chunks):
    cat = jnp.concatenate(
        [
            jnp.concatenate(
                [flat[pl.ds(slot_row(block, r), 16), k * 128 : (k + 1) * 128] for k in range(TILES)],
                axis=0,
            )
            for r in range(CAP)
        ],
        axis=1,
    )
    out = dot(perm, cat).astype(BF16)
    for r in range(CAP):
        chunks[pl.ds(block * 16, 16), r] = out[:, r * 128 : (r + 1) * 128].reshape(16, TILES, 128)


def unpack_block(block, perm, chunks, flat):
    cat = jnp.concatenate(
        [chunks[pl.ds(block * 16, 16), r].reshape(256, 128) for r in range(CAP)], axis=1
    )
    out = dot(perm, cat).astype(BF16)
    for r in range(CAP):
        for k in range(TILES):
            flat[pl.ds(slot_row(block, r), 16), k * 128 : (k + 1) * 128] = out[
                k * 16 : (k + 1) * 16, r * 128 : (r + 1) * 128
            ]


def layer_kernel(
    q_ref,
    k_ref,
    v_ref,
    o_ref,
    g_ref,
    log_ref,
    order_ref,
    rows_ref,
    mgrad_ref,
    ids_ref,
    gate_ref,
    wg_hbm,
    wu_hbm,
    wd_hbm,
    dq_ref,
    dk_ref,
    dv_ref,
    drows_ref,
    dgates_ref,
    gg_hbm,
    gu_hbm,
    gd_hbm,
    kv_own,
    kvb,
    dkb,
    rsb,
    qb,
    gb,
    st,
    dqs,
    dqr,
    perm_ref,
    send_a,
    send_b,
    recv_a,
    recv_b,
    back,
    gt_send,
    gt_recv,
    xb,
    yb,
    slb,
    wg,
    wu,
    wd,
    act_g,
    act_u,
    gub,
    hb,
    out_a,
    out_b,
    out_d,
    w_sem,
    out_sem,
    kv_sem,
    q_sem,
    a_sem,
    b_sem,
    rs_sem,
    dq_sem,
    ret_sem,
    gt_sem,
):
    c = lax.axis_index("ctx")
    k = lax.axis_index("kv")
    me = c * 2 + k
    chip = c // 2
    core = lax.rem(c, 2)
    other = chip * 2 + 1 - core
    score_scale = 1.0 / math.sqrt(128.0)

    weights = [
        pltpu.make_async_copy(src, dst, w_sem.at[i])
        for i, (src, dst) in enumerate(((wg_hbm, wg), (wu_hbm, wu), (wd_hbm, wd)))
    ]
    for copy in weights:
        copy.start()

    barrier = pltpu.get_barrier_semaphore()

    def greet(step, carry):
        pc, pk = any_partner(step, c, k)
        pl.semaphore_signal(barrier, inc=1, device_id=(pc, pk), device_id_type=MESH)
        return carry

    lax.fori_loop(1, DEVS, greet, 0)

    for h in range(2):
        kv_own[h, :, 0:128] = k_ref[h * HALF : (h + 1) * HALF, :]
        kv_own[h, :, 128:256] = v_ref[h * HALF : (h + 1) * HALF, :]
    qb[0] = q_ref[...]
    gb[0] = g_ref[...]
    prod = g_ref[...].astype(F32) * o_ref[...].astype(F32)
    hi = prod.astype(BF16)
    mid = (prod - hi.astype(F32)).astype(BF16)
    ones = jnp.ones((8, 128), BF16)
    delta = dot_nt(ones, hi) + dot_nt(ones, mid)
    row8 = lax.broadcasted_iota(jnp.int32, (8, 1024), 0)
    st[0] = jnp.where(row8 == 0, log_ref[...] * LOG2E, delta)

    lane = lax.broadcasted_iota(jnp.int32, (HALF, DEVS), 1)
    ids = ids_ref[...]
    gates = gate_ref[...].astype(F32)
    hits = [(ids[:, j : j + 1] == lane).astype(F32) for j in range(8)]
    named = functools.reduce(jnp.add, hits)
    gate_of = functools.reduce(jnp.add, [hits[j] * gates[:, j : j + 1] for j in range(8)])
    below = (
        lax.broadcasted_iota(jnp.int32, (HALF, HALF), 0)
        > lax.broadcasted_iota(jnp.int32, (HALF, HALF), 1)
    ).astype(BF16)
    rank = dot(below, named.astype(BF16))
    picks = [jnp.where(rank == float(r), named, 0.0) for r in range(CAP)]
    ri = lax.broadcasted_iota(jnp.int32, (256, 256), 0)
    ci = lax.broadcasted_iota(jnp.int32, (256, 256), 1)
    perm_ref[...] = (
        jnp.where(ri // 16 == lax.rem(ci, 16), 1.0, 0.0)
        * jnp.where(lax.rem(ri, 16) == ci // 16, 1.0, 0.0)
    ).astype(BF16)

    pl.semaphore_wait(barrier, DEVS - 1)

    def send_kv(step, carry):
        chip_to = chip_partner(step, c)
        pltpu.make_async_remote_copy(
            src_ref=kv_own,
            dst_ref=kvb.at[chip],
            send_sem=kv_sem.at[0],
            recv_sem=kv_sem.at[1],
            device_id=(chip_to * 2 + core, k),
            device_id_type=MESH,
        ).start()
        return carry

    to_core = [
        pltpu.make_async_remote_copy(
            src_ref=buf.at[0],
            dst_ref=buf.at[1],
            send_sem=q_sem.at[i],
            recv_sem=q_sem.at[3 + i],
            device_id=(other, k),
            device_id_type=MESH,
        )
        for i, buf in enumerate((qb, gb, st))
    ]
    for copy in to_core:
        copy.start()
    lax.fori_loop(1, CHIPS, send_kv, 0)
    kvb[pl.ds(chip, 1)] = kv_own[...].reshape(1, 2, HALF, 256)

    def dispatch(values, tables, flat, chunks, got, sems):
        for r in range(CAP):
            table = tables[r].astype(BF16)
            for n in range(4):
                part = dot_tn(table, values[:, n * 512 : (n + 1) * 512]).astype(BF16)
                for h in range(2):
                    flat[h * 320 + r * 64 : h * 320 + r * 64 + 64, n * 512 : (n + 1) * 512] = part[
                        h * 64 : (h + 1) * 64
                    ]

        def pack(block, carry):
            pack_block(block, perm_ref[...], flat, chunks)
            return carry

        lax.fori_loop(0, 8, pack, 0)

        send_all(chunks, got, sems)
        got[pl.ds(me, 1)] = chunks[pl.ds(me, 1)]

    def send_all(chunks, got, sems):
        def send(step, carry):
            pc, pk = any_partner(step, c, k)
            pltpu.make_async_remote_copy(
                src_ref=chunks.at[pc * 2 + pk],
                dst_ref=got.at[me],
                send_sem=sems.at[0],
                recv_sem=sems.at[1],
                device_id=(pc, pk),
                device_id_type=MESH,
            ).start()
            return carry

        lax.fori_loop(1, DEVS, send, 0)

    def wait_all(buf, sem, count):
        part = buf.at[pl.ds(0, count)]
        pltpu.make_async_copy(part, part, sem).wait()

    dispatch(rows_ref, picks, xb, send_a, recv_a, a_sem)
    dispatch(
        mgrad_ref,
        [jnp.where(p > 0.0, gate_of, 0.0) for p in picks],
        yb,
        send_b,
        recv_b,
        b_sem,
    )

    for copy in to_core:
        copy.wait()
    wait_all(kvb, kv_sem.at[0], CHIPS - 1)
    wait_all(kvb, kv_sem.at[1], CHIPS - 1)
    gap = (
        lax.broadcasted_iota(jnp.int32, (HALF, 512), 0)
        - lax.broadcasted_iota(jnp.int32, (HALF, 512), 1) // 8
    )
    dqs[...] = jnp.zeros_like(dqs)

    def key_tile(i, carry):
        for late_key in range(2):
            kv = kvb[pl.ds(i * 4, 4), late_key].reshape(256, 256)
            key_part = kv[:, 0:128]
            value_part = kv[:, 128:256]
            dk_sum = jnp.zeros((256, 128), F32)
            dv_sum = jnp.zeros((256, 128), F32)
            for late_q in range(late_key, 2):
                for who in range(2):
                    span = slice(late_q * 512, (late_q + 1) * 512)
                    qs = qb[who, span, :]
                    gs = gb[who, span, :]
                    shifted = dot_nt(key_part, qs) * (score_scale * LOG2E) - st[who, 0:1, span]
                    if late_q == late_key:
                        owner = c if who == 0 else other
                        own_stretch = order_ref[2 * owner + late_q]
                        pieces = []
                        for s in range(4):
                            key_stretch = order_ref[2 * ((i * 4 + s) * 2 + core) + late_key]
                            room = (own_stretch - key_stretch) * HALF
                            pieces.append(
                                jnp.where(gap <= room, shifted[s * HALF : (s + 1) * HALF], -1e30)
                            )
                        shifted = jnp.concatenate(pieces, axis=0)
                    probs = jnp.exp2(shifted)
                    dv_sum = dv_sum + dot(probs.astype(BF16), gs)
                    d_scores = (probs * (dot_nt(value_part, gs) - st[who, 1:2, span])).astype(BF16)
                    dk_sum = dk_sum + dot(d_scores, qs)
                    dqs[who, :, span] += dot_tn(key_part, d_scores)
            both = jnp.concatenate([dk_sum * score_scale, dv_sum], axis=1).astype(BF16)
            dkb[pl.ds(i * 4, 4), late_key] = both.reshape(4, HALF, 256)
        return carry

    lax.fori_loop(0, CHIPS // 4, key_tile, 0)

    dq_copy = pltpu.make_async_remote_copy(
        src_ref=dqs.at[1],
        dst_ref=dqr,
        send_sem=dq_sem.at[0],
        recv_sem=dq_sem.at[1],
        device_id=(other, k),
        device_id_type=MESH,
    )
    dq_copy.start()

    def send_partial(step, carry):
        chip_to = chip_partner(step, c)
        pltpu.make_async_remote_copy(
            src_ref=dkb.at[chip_to],
            dst_ref=rsb.at[chip],
            send_sem=rs_sem.at[0],
            recv_sem=rs_sem.at[1],
            device_id=(chip_to * 2 + core, k),
            device_id_type=MESH,
        ).start()
        return carry

    lax.fori_loop(1, CHIPS, send_partial, 0)
    rsb[pl.ds(chip, 1)] = dkb[pl.ds(chip, 1)]

    def unpack(chunks, flat):
        def body(block, carry):
            unpack_block(block, perm_ref[...], chunks, flat)
            return carry

        lax.fori_loop(0, 8, body, 0)

    wait_all(recv_a, a_sem.at[1], DEVS - 1)
    unpack(recv_a, xb)
    weights[0].wait()
    weights[1].wait()

    def gate_up(n, carry):
        cols = pl.ds(pl.multiple_of(n * 256, 256), 256)
        act_g[:, cols] = dot(xb[...], wg[:, cols])
        act_u[:, cols] = dot(xb[...], wu[:, cols])
        return carry

    lax.fori_loop(0, 3, gate_up, 0)
    weights[2].wait()
    wait_all(send_a, a_sem.at[0], DEVS - 1)
    wait_all(recv_b, b_sem.at[1], DEVS - 1)
    unpack(recv_b, yb)

    def hidden_part(n, gate_sum):
        cols = pl.ds(pl.multiple_of(n * 256, 256), 256)
        cols_up = pl.ds(pl.multiple_of(n * 256 + 768, 256), 256)
        projected = dot_nt(yb[...], wd[cols, :])
        ga = act_g[:, cols]
        ua = act_u[:, cols]
        sig = jax.nn.sigmoid(ga)
        silu = ga * sig
        hidden = (silu * ua).astype(BF16)
        hb[:, cols] = hidden
        gub[:, cols] = (projected * ua * sig * (1.0 + ga * (1.0 - sig))).astype(BF16)
        gub[:, cols_up] = (projected * silu).astype(BF16)
        return gate_sum + jnp.sum(projected * hidden.astype(F32), axis=1, keepdims=True)

    gate_sum = lax.fori_loop(0, 3, hidden_part, jnp.zeros((640, 1), F32))
    lane_h = lax.broadcasted_iota(jnp.int32, (HALF, 128), 1)
    for h in range(2):
        tile = jnp.zeros((HALF, 128), F32)
        for r in range(CAP):
            first = h * 320 + r * 64
            tile = jnp.where(lane_h == r, gate_sum[first : first + 64], tile)
        gt_send[h * HALF : (h + 1) * HALF] = jnp.broadcast_to(
            tile[:, None, :], (HALF, 16, 128)
        ).astype(BF16)
    send_all(gt_send, gt_recv, gt_sem)
    gt_recv[pl.ds(me, 1)] = gt_send[pl.ds(me, 1)]

    def slot_cols(n, carry):
        cols = pl.ds(pl.multiple_of(n * 256, 256), 256)
        slb[:, cols] = (
            dot_nt(gub[:, 0:768], wg[cols, :]) + dot_nt(gub[:, 768:1536], wu[cols, :])
        ).astype(BF16)
        return carry

    lax.fori_loop(0, 8, slot_cols, 0)

    def pack_back(block, carry):
        pack_block(block, perm_ref[...], slb, send_a)
        return carry

    lax.fori_loop(0, 8, pack_back, 0)
    send_all(send_a, back, ret_sem)
    back[pl.ds(me, 1)] = send_a[pl.ds(me, 1)]

    def grad_in(n, carry):
        rows = pl.ds(pl.multiple_of(n * 256, 256), 256)
        out_a[rows, :] = dot_tn(xb[:, rows], gub[:, 0:768]).astype(BF16)
        out_b[rows, :] = dot_tn(xb[:, rows], gub[:, 768:1536]).astype(BF16)
        return carry

    lax.fori_loop(0, 8, grad_in, 0)
    outs = [
        pltpu.make_async_copy(src, dst, out_sem.at[i])
        for i, (src, dst) in enumerate(((out_a, gg_hbm), (out_b, gu_hbm), (out_d, gd_hbm)))
    ]
    outs[0].start()
    outs[1].start()

    def grad_out(n, carry):
        cols = pl.ds(pl.multiple_of(n * 512, 512), 512)
        out_d[:, cols] = dot_tn(hb[...], yb[:, cols]).astype(BF16)
        return carry

    lax.fori_loop(0, 4, grad_out, 0)
    outs[2].start()

    wait_all(dkb, rs_sem.at[0], CHIPS - 1)
    wait_all(rsb, rs_sem.at[1], CHIPS - 1)

    def add_up(j, total):
        return total + rsb[j].astype(F32)

    total = lax.fori_loop(0, CHIPS, add_up, jnp.zeros((2, HALF, 256), F32))
    for h in range(2):
        dk_ref[h * HALF : (h + 1) * HALF, :] = total[h, :, 0:128].astype(BF16)
        dv_ref[h * HALF : (h + 1) * HALF, :] = total[h, :, 128:256].astype(BF16)
    dq_copy.wait()
    dq_ref[...] = jnp.transpose((dqs[0] + dqr[...]) * score_scale).astype(BF16)

    wait_all(gt_send, gt_sem.at[0], DEVS - 1)
    wait_all(gt_recv, gt_sem.at[1], DEVS - 1)
    slot_gates = jnp.transpose(gt_recv[...].astype(F32)[:, 0, :])
    gate_grads = functools.reduce(
        jnp.add, [picks[r] * slot_gates[r : r + 1, :] for r in range(CAP)]
    )
    lane8 = lax.broadcasted_iota(jnp.int32, (HALF, 8), 1)
    d_gates = jnp.zeros((HALF, 8), F32)
    for j in range(8):
        d_gates = jnp.where(
            lane8 == j, jnp.sum(hits[j] * gate_grads, axis=1, keepdims=True), d_gates
        )
    dgates_ref[...] = (d_gates / gates).astype(BF16)

    wait_all(send_b, b_sem.at[0], DEVS - 1)
    wait_all(send_a, ret_sem.at[0], DEVS - 1)
    wait_all(back, ret_sem.at[1], DEVS - 1)
    unpack(back, slb)
    tables = [picks[r].astype(BF16) for r in range(CAP)]

    def combine(n, carry):
        cols = pl.ds(pl.multiple_of(n * 512, 512), 512)
        acc = jnp.zeros((HALF, 512), F32)
        for r in range(CAP):
            for h in range(2):
                acc = acc + dot(
                    tables[r][:, h * 64 : (h + 1) * 64],
                    slb[h * 320 + r * 64 : h * 320 + r * 64 + 64, cols],
                )
        drows_ref[:, cols] = acc.astype(BF16)
        return carry

    lax.fori_loop(0, 4, combine, 0)
    for copy in outs:
        copy.wait()


def shards(
    query_rows,
    key_rows,
    value_rows,
    attn_out,
    attn_grad,
    log_total,
    stretch_order,
    moe_rows,
    moe_grad,
    expert_ids,
    gate_prob,
    gate_weight,
    up_weight,
    down_weight,
):
    tok, heads, size = query_rows.shape
    flat = tok * heads
    rows_here, width = moe_rows.shape
    hidden = gate_weight.shape[2]
    vmem = pl.BlockSpec(memory_space=pltpu.VMEM)
    smem = pl.BlockSpec(memory_space=pltpu.SMEM)
    hbm = pl.BlockSpec(memory_space=pl.ANY)
    chunk = (DEVS, CAP, TILES, 128)
    slots = DEVS * CAP
    results = pl.pallas_call(
        layer_kernel,
        out_shape=(
            jax.ShapeDtypeStruct((flat, size), BF16),
            jax.ShapeDtypeStruct((tok, size), BF16),
            jax.ShapeDtypeStruct((tok, size), BF16),
            jax.ShapeDtypeStruct((rows_here, width), BF16),
            jax.ShapeDtypeStruct((rows_here, 8), BF16),
            jax.ShapeDtypeStruct((width, hidden), BF16),
            jax.ShapeDtypeStruct((width, hidden), BF16),
            jax.ShapeDtypeStruct((hidden, width), BF16),
        ),
        in_specs=[vmem] * 6 + [smem] + [vmem] * 4 + [hbm] * 3,
        out_specs=(vmem,) * 5 + (hbm,) * 3,
        scratch_shapes=[
            pltpu.VMEM((2, HALF, 256), BF16),
            pltpu.VMEM((CHIPS, 2, HALF, 256), BF16),
            pltpu.VMEM((CHIPS, 2, HALF, 256), BF16),
            pltpu.VMEM((CHIPS, 2, HALF, 256), BF16),
            pltpu.VMEM((2, flat, size), BF16),
            pltpu.VMEM((2, flat, size), BF16),
            pltpu.VMEM((2, 8, flat), F32),
            pltpu.VMEM((2, size, flat), F32),
            pltpu.VMEM((size, flat), F32),
            pltpu.VMEM((256, 256), BF16),
            pltpu.VMEM(chunk, BF16),
            pltpu.VMEM(chunk, BF16),
            pltpu.VMEM(chunk, BF16),
            pltpu.VMEM(chunk, BF16),
            pltpu.VMEM(chunk, BF16),
            pltpu.VMEM((DEVS, 16, 128), BF16),
            pltpu.VMEM((DEVS, 16, 128), BF16),
            pltpu.VMEM((slots, width), BF16),
            pltpu.VMEM((slots, width), BF16),
            pltpu.VMEM((slots, width), BF16),
            pltpu.VMEM((width, hidden), BF16),
            pltpu.VMEM((width, hidden), BF16),
            pltpu.VMEM((hidden, width), BF16),
            pltpu.VMEM((slots, hidden), F32),
            pltpu.VMEM((slots, hidden), F32),
            pltpu.VMEM((slots, 2 * hidden), BF16),
            pltpu.VMEM((slots, hidden), BF16),
            pltpu.VMEM((width, hidden), BF16),
            pltpu.VMEM((width, hidden), BF16),
            pltpu.VMEM((hidden, width), BF16),
            pltpu.SemaphoreType.DMA((3,)),
            pltpu.SemaphoreType.DMA((3,)),
            pltpu.SemaphoreType.DMA((2,)),
            pltpu.SemaphoreType.DMA((6,)),
            pltpu.SemaphoreType.DMA((2,)),
            pltpu.SemaphoreType.DMA((2,)),
            pltpu.SemaphoreType.DMA((2,)),
            pltpu.SemaphoreType.DMA((2,)),
            pltpu.SemaphoreType.DMA((2,)),
            pltpu.SemaphoreType.DMA((2,)),
        ],
        compiler_params=pltpu.CompilerParams(
            collective_id=0, has_side_effects=True, vmem_limit_bytes=62 * 1024 * 1024
        ),
    )(
        query_rows.reshape(flat, size),
        key_rows.reshape(tok, size),
        value_rows.reshape(tok, size),
        attn_out.reshape(flat, size),
        attn_grad.reshape(flat, size),
        log_total.reshape(1, flat),
        stretch_order,
        moe_rows,
        moe_grad,
        expert_ids,
        gate_prob,
        gate_weight[0],
        up_weight[0],
        down_weight[0],
    )
    d_query, d_key, d_value, d_rows, d_gates, grad_gate, grad_up, grad_down = results
    return (
        d_query.reshape(tok, heads, size),
        d_key.reshape(tok, 1, size),
        d_value.reshape(tok, 1, size),
        d_rows,
        d_gates,
        grad_gate[None],
        grad_up[None],
        grad_down[None],
    )


def solution(mesh):
    both = ("ctx", "kv")
    heads = P("ctx", "kv", None)
    tokens = P(both, None)
    experts = P(both, None, None)
    return jax.shard_map(
        shards,
        mesh=mesh,
        in_specs=(heads,) * 5
        + (P("ctx", "kv"), P())
        + (tokens,) * 4
        + (experts,) * 3,
        out_specs=(heads,) * 3 + (tokens,) * 2 + (experts,) * 3,
        check_vma=False,
    )
```

```python
import functools
import math

import jax
import jax.numpy as jnp
from jax import lax
from jax.experimental import pallas as pl
from jax.experimental.pallas import tpu as pltpu
from jax.sharding import PartitionSpec as P

MESH = pl.DeviceIdType.MESH
LOG2E = 1.4426950408889634
F32 = jnp.float32
BF16 = jnp.bfloat16
CAP = 5
TILES = 16
DEVS = 128
CHIPS = 32
HALF = 64


def chip_step(step, c, k):
    s = lax.rem(step * 29, 64)
    x = lax.rem(c // 16 + lax.rem(s, 4), 4)
    s = s // 4
    y = lax.rem(lax.rem(c // 4, 4) + lax.rem(s, 4), 4)
    z = lax.rem(lax.rem(c // 2, 2) * 2 + k + s // 4, 4)
    return (x * 4 + y) * 2 + z // 2, lax.rem(z, 2)


def any_partner(step, c, k):
    chip, kk = chip_step(step // 2, c, k)
    return chip * 2 + lax.rem(lax.rem(c, 2) + lax.rem(step, 2), 2), kk


def place(c, k):
    return lax.rem(c, 2) * 64 + (c // 2) * 2 + k


def dot(a, b):
    return jnp.dot(a, b, preferred_element_type=F32)


def dot_nt(a, b):
    return lax.dot_general(a, b, (((1,), (1,)), ((), ())), preferred_element_type=F32)


def dot_tn(a, b):
    return lax.dot_general(a, b, (((0,), (0,)), ((), ())), preferred_element_type=F32)


def slot_row(block, r):
    return pl.multiple_of((block // 4) * (CAP * HALF) + r * HALF + lax.rem(block, 4) * 16, 16)


def pack_block(block, perm, flat, chunks):
    cat = jnp.concatenate(
        [
            jnp.concatenate(
                [flat[pl.ds(slot_row(block, r), 16), k * 128 : (k + 1) * 128] for k in range(TILES)],
                axis=0,
            )
            for r in range(CAP)
        ],
        axis=1,
    )
    out = dot(perm, cat).astype(BF16)
    for r in range(CAP):
        chunks[pl.ds(block * 16, 16), r] = out[:, r * 128 : (r + 1) * 128].reshape(16, TILES, 128)


def unpack_block(block, perm, chunks, flat):
    cat = jnp.concatenate(
        [chunks[pl.ds(block * 16, 16), r].reshape(256, 128) for r in range(CAP)], axis=1
    )
    out = dot(perm, cat).astype(BF16)
    for r in range(CAP):
        for k in range(TILES):
            flat[pl.ds(slot_row(block, r), 16), k * 128 : (k + 1) * 128] = out[
                k * 16 : (k + 1) * 16, r * 128 : (r + 1) * 128
            ]


def layer_kernel(
    q_ref,
    k_ref,
    v_ref,
    o_ref,
    g_ref,
    log_ref,
    order_ref,
    rows_ref,
    mgrad_ref,
    ids_ref,
    gate_ref,
    wg_hbm,
    wu_hbm,
    wd_hbm,
    dq_ref,
    dk_ref,
    dv_ref,
    drows_ref,
    dgates_ref,
    gg_hbm,
    gu_hbm,
    gd_hbm,
    kv_own,
    kvb,
    dkb,
    rs1,
    mid,
    rs2,
    table,
    gtable,
    qb,
    gb,
    st,
    dqs,
    dqr,
    perm_ref,
    send_a,
    send_b,
    recv_a,
    recv_b,
    back,
    gt_send,
    gt_recv,
    xb,
    yb,
    slb,
    wg,
    wu,
    wd,
    act_g,
    act_u,
    gub,
    hb,
    out_a,
    out_b,
    out_d,
    w_sem,
    out_sem,
    kv_sem,
    q_sem,
    a_sem,
    b_sem,
    rs_sem,
    dq_sem,
    ret_sem,
    gt_sem,
):
    c = lax.axis_index("ctx")
    k = lax.axis_index("kv")
    me = place(c, k)
    chip = c // 2
    core = lax.rem(c, 2)
    other = chip * 2 + 1 - core
    zh = lax.rem(chip, 2)
    at_x = chip // 8
    at_y = lax.rem(chip // 2, 4)
    at_b = at_x * (1 - core) + at_y * core
    at_m = at_y * (1 - core) + at_x * core
    step_b = 8 - 6 * core
    step_m = 2 + 6 * core
    score_scale = 1.0 / math.sqrt(128.0)

    weights = [
        pltpu.make_async_copy(src, dst, w_sem.at[i])
        for i, (src, dst) in enumerate(((wg_hbm, wg), (wu_hbm, wu), (wd_hbm, wd)))
    ]
    for copy in weights:
        copy.start()

    barrier = pltpu.get_barrier_semaphore()

    def greet(step, carry):
        pc, pk = any_partner(step, c, k)
        pl.semaphore_signal(barrier, inc=1, device_id=(pc, pk), device_id_type=MESH)
        return carry

    lax.fori_loop(1, DEVS, greet, 0)

    for h in range(2):
        kv_own[h, :, 0:128] = k_ref[h * HALF : (h + 1) * HALF, :]
        kv_own[h, :, 128:256] = v_ref[h * HALF : (h + 1) * HALF, :]
    qb[0] = q_ref[...]
    gb[0] = g_ref[...]
    prod = g_ref[...].astype(F32) * o_ref[...].astype(F32)
    hi = prod.astype(BF16)
    low = (prod - hi.astype(F32)).astype(BF16)
    ones = jnp.ones((8, 128), BF16)
    delta = dot_nt(ones, hi) + dot_nt(ones, low)
    logs = log_ref[...]
    log_hi = logs.astype(BF16)
    rest = logs - log_hi.astype(F32)
    log_mid = rest.astype(BF16)
    log_low = (rest - log_mid.astype(F32)).astype(BF16)
    spread = (
        lax.broadcasted_iota(jnp.int32, (128, 1024), 1) // 8
        == lax.broadcasted_iota(jnp.int32, (128, 1024), 0)
    ).astype(BF16)
    wide = dot(log_hi, spread) + dot(log_mid, spread) + dot(log_low, spread)
    row8 = lax.broadcasted_iota(jnp.int32, (8, 1024), 0)
    mine = row8 == lax.rem(lax.broadcasted_iota(jnp.int32, (8, 1024), 1), 8)
    log_row = jnp.sum(jnp.where(mine, wide, 0.0), axis=0, keepdims=True)
    st[0] = jnp.where(row8 == 0, log_row * LOG2E, delta)

    spot = lax.broadcasted_iota(jnp.int32, (DEVS, HALF), 0)
    expert = (lax.rem(spot, 64) // 2) * 4 + (spot // 64) * 2 + lax.rem(spot, 2)
    gates = gate_ref[...].astype(F32)

    def hit(j):
        return jnp.where(expert == ids_ref[j : j + 1, :], 1.0, 0.0)

    named = functools.reduce(jnp.add, [hit(j) for j in range(8)])
    gate_of = functools.reduce(jnp.add, [hit(j) * gates[j : j + 1, :] for j in range(8)])
    before = (
        lax.broadcasted_iota(jnp.int32, (HALF, HALF), 0)
        < lax.broadcasted_iota(jnp.int32, (HALF, HALF), 1)
    ).astype(BF16)
    rank = dot(named.astype(BF16), before)
    for r in range(CAP):
        pick = jnp.where(rank == float(r), named, 0.0)
        scaled = (pick * gate_of).astype(BF16)
        pick = pick.astype(BF16)
        for h in range(2):
            first = h * 320 + r * 64
            table[first : first + 64, :] = pick[h * 64 : (h + 1) * 64]
            gtable[first : first + 64, :] = scaled[h * 64 : (h + 1) * 64]
    ri = lax.broadcasted_iota(jnp.int32, (256, 256), 0)
    ci = lax.broadcasted_iota(jnp.int32, (256, 256), 1)
    perm_ref[...] = (
        jnp.where(ri // 16 == lax.rem(ci, 16), 1.0, 0.0)
        * jnp.where(lax.rem(ri, 16) == ci // 16, 1.0, 0.0)
    ).astype(BF16)

    def gather(values, chosen, flat, chunks):
        def cols(n, carry):
            span = pl.ds(pl.multiple_of(n * 512, 512), 512)
            flat[:, span] = dot(chosen[...], values[:, span]).astype(BF16)
            return carry

        lax.fori_loop(0, 4, cols, 0)

        def pack(block, carry):
            pack_block(block, perm_ref[...], flat, chunks)
            return carry

        lax.fori_loop(0, 8, pack, 0)

    def send_to(pc, pk, chunks, got, sems):
        pltpu.make_async_remote_copy(
            src_ref=chunks.at[place(pc, pk)],
            dst_ref=got.at[me],
            send_sem=sems.at[0],
            recv_sem=sems.at[1],
            device_id=(pc, pk),
            device_id_type=MESH,
        ).start()

    def send_all(chunks, got, sems):
        def send(step, carry):
            pc, pk = any_partner(step, c, k)
            send_to(pc, pk, chunks, got, sems)
            return carry

        lax.fori_loop(1, DEVS, send, 0)

    def wait_all(buf, sem, count):
        part = buf.at[pl.ds(0, count)]
        pltpu.make_async_copy(part, part, sem).wait()

    gather(rows_ref, table, xb, send_a)

    pl.semaphore_wait(barrier, DEVS - 1)

    to_core = [
        pltpu.make_async_remote_copy(
            src_ref=buf.at[0],
            dst_ref=buf.at[1],
            send_sem=q_sem.at[i],
            recv_sem=q_sem.at[3 + i],
            device_id=(other, k),
            device_id_type=MESH,
        )
        for i, buf in enumerate((qb, gb, st))
    ]
    for copy in to_core:
        copy.start()

    def near(step):
        return lax.rem(at_m + lax.rem(step, 4), 4), lax.rem(zh + step // 4, 2)

    def send_kv(step, carry):
        m, z = near(step)
        pltpu.make_async_remote_copy(
            src_ref=kv_own,
            dst_ref=kvb.at[chip],
            send_sem=kv_sem.at[0],
            recv_sem=kv_sem.at[1],
            device_id=((at_b * step_b + m * step_m + z) * 2 + core, k),
            device_id_type=MESH,
        ).start()
        return carry

    lax.fori_loop(1, 8, send_kv, 0)
    send_all(send_a, recv_a, a_sem)
    recv_a[pl.ds(me, 1)] = send_a[pl.ds(me, 1)]
    kvb[pl.ds(chip, 1)] = kv_own[...].reshape(1, 2, HALF, 256)
    wait_all(kvb, kv_sem.at[1], 7)

    def pass_kv(step, carry):
        b = lax.rem(at_b + 1 + lax.rem(step, 3), 4)
        i = step // 3
        block = at_b * step_b + (i // 2) * step_m + lax.rem(i, 2)
        pltpu.make_async_remote_copy(
            src_ref=kvb.at[block],
            dst_ref=kvb.at[block],
            send_sem=kv_sem.at[2],
            recv_sem=kv_sem.at[3],
            device_id=((b * step_b + at_m * step_m + zh) * 2 + core, k),
            device_id_type=MESH,
        ).start()
        return carry

    lax.fori_loop(0, 24, pass_kv, 0)

    gather(mgrad_ref, gtable, yb, send_b)
    send_all(send_b, recv_b, b_sem)
    recv_b[pl.ds(me, 1)] = send_b[pl.ds(me, 1)]

    for copy in to_core:
        copy.wait()
    wait_all(kvb, kv_sem.at[0], 7)
    wait_all(kvb, kv_sem.at[2], 24)
    wait_all(kvb, kv_sem.at[3], 24)
    gap = (
        lax.broadcasted_iota(jnp.int32, (HALF, 512), 0)
        - lax.broadcasted_iota(jnp.int32, (HALF, 512), 1) // 8
    )
    dqs[...] = jnp.zeros_like(dqs)

    def key_tile(i, carry):
        for late_key in range(2):
            kv = kvb[pl.ds(i * 4, 4), late_key].reshape(256, 256)
            key_part = kv[:, 0:128]
            value_part = kv[:, 128:256]
            dk_sum = jnp.zeros((256, 128), F32)
            dv_sum = jnp.zeros((256, 128), F32)
            for late_q in range(late_key, 2):
                for who in range(2):
                    span = slice(late_q * 512, (late_q + 1) * 512)
                    qs = qb[who, span, :]
                    gs = gb[who, span, :]
                    shifted = dot_nt(key_part, qs) * (score_scale * LOG2E) - st[who, 0:1, span]
                    if late_q == late_key:
                        owner = c if who == 0 else other
                        own_stretch = order_ref[2 * owner + late_q]
                        pieces = []
                        for s in range(4):
                            key_stretch = order_ref[2 * ((i * 4 + s) * 2 + core) + late_key]
                            room = (own_stretch - key_stretch) * HALF
                            pieces.append(
                                jnp.where(gap <= room, shifted[s * HALF : (s + 1) * HALF], -1e30)
                            )
                        shifted = jnp.concatenate(pieces, axis=0)
                    probs = jnp.exp2(shifted)
                    dv_sum = dv_sum + dot(probs.astype(BF16), gs)
                    d_scores = (probs * (dot_nt(value_part, gs) - st[who, 1:2, span])).astype(BF16)
                    dk_sum = dk_sum + dot(d_scores, qs)
                    dqs[who, :, span] += dot_tn(key_part, d_scores)
            both = jnp.concatenate([dk_sum * score_scale, dv_sum], axis=1).astype(BF16)
            dkb[pl.ds(i * 4, 4), late_key] = both.reshape(4, HALF, 256)
        return carry

    lax.fori_loop(0, CHIPS // 4, key_tile, 0)

    dq_copy = pltpu.make_async_remote_copy(
        src_ref=dqs.at[1],
        dst_ref=dqr,
        send_sem=dq_sem.at[0],
        recv_sem=dq_sem.at[1],
        device_id=(other, k),
        device_id_type=MESH,
    )
    dq_copy.start()

    def send_partial(step, carry):
        shift = 1 + lax.rem(step, 3)
        b = lax.rem(at_b + shift, 4)
        i = step // 3
        pltpu.make_async_remote_copy(
            src_ref=dkb.at[b * step_b + (i // 2) * step_m + lax.rem(i, 2)],
            dst_ref=rs1.at[(shift - 1) * 8 + i],
            send_sem=rs_sem.at[0],
            recv_sem=rs_sem.at[1],
            device_id=((b * step_b + at_m * step_m + zh) * 2 + core, k),
            device_id_type=MESH,
        ).start()
        return carry

    def send_mid(step, carry):
        m, z = near(step)
        pltpu.make_async_remote_copy(
            src_ref=mid.at[m * 2 + z],
            dst_ref=rs2.at[step - 1],
            send_sem=rs_sem.at[2],
            recv_sem=rs_sem.at[3],
            device_id=((at_b * step_b + m * step_m + z) * 2 + core, k),
            device_id_type=MESH,
        ).start()
        return carry

    def unpack(chunks, flat):
        def body(block, carry):
            unpack_block(block, perm_ref[...], chunks, flat)
            return carry

        lax.fori_loop(0, 8, body, 0)

    wait_all(recv_a, a_sem.at[1], DEVS - 1)
    unpack(recv_a, xb)
    weights[0].wait()
    weights[1].wait()

    def gate_up(n, carry):
        cols = pl.ds(pl.multiple_of(n * 256, 256), 256)
        act_g[:, cols] = dot(xb[...], wg[:, cols])
        act_u[:, cols] = dot(xb[...], wu[:, cols])
        return carry

    lax.fori_loop(0, 3, gate_up, 0)
    weights[2].wait()
    wait_all(send_a, a_sem.at[0], DEVS - 1)
    wait_all(recv_b, b_sem.at[1], DEVS - 1)
    lax.fori_loop(0, 24, send_partial, 0)
    unpack(recv_b, yb)

    def hidden_part(n, gate_sum):
        cols = pl.ds(pl.multiple_of(n * 256, 256), 256)
        cols_up = pl.ds(pl.multiple_of(n * 256 + 768, 256), 256)
        projected = dot_nt(yb[...], wd[cols, :])
        ga = act_g[:, cols]
        ua = act_u[:, cols]
        sig = jax.nn.sigmoid(ga)
        silu = ga * sig
        hidden = (silu * ua).astype(BF16)
        hb[:, cols] = hidden
        gub[:, cols] = (projected * ua * sig * (1.0 + ga * (1.0 - sig))).astype(BF16)
        gub[:, cols_up] = (projected * silu).astype(BF16)
        return gate_sum + jnp.sum(projected * hidden.astype(F32), axis=1, keepdims=True)

    gate_sum = lax.fori_loop(0, 3, hidden_part, jnp.zeros((640, 1), F32))
    lane_h = lax.broadcasted_iota(jnp.int32, (HALF, 128), 1)
    for h in range(2):
        tile = jnp.zeros((HALF, 128), F32)
        for r in range(CAP):
            first = h * 320 + r * 64
            tile = jnp.where(lane_h == r, gate_sum[first : first + 64], tile)
        gt_send[h * HALF : (h + 1) * HALF] = jnp.broadcast_to(
            tile[:, None, :], (HALF, 16, 128)
        ).astype(BF16)
    send_all(gt_send, gt_recv, gt_sem)
    gt_recv[pl.ds(me, 1)] = gt_send[pl.ds(me, 1)]

    for h in range(2):
        span = slice(h * 320, (h + 1) * 320)

        def slot_cols(n, carry):
            cols = pl.ds(pl.multiple_of(n * 256, 256), 256)
            slb[span, cols] = (
                dot_nt(gub[span, 0:768], wg[cols, :]) + dot_nt(gub[span, 768:1536], wu[cols, :])
            ).astype(BF16)
            return carry

        lax.fori_loop(0, 8, slot_cols, 0)

        def pack_back(block, carry):
            pack_block(block, perm_ref[...], slb, send_a)
            return carry

        lax.fori_loop(h * 4, h * 4 + 4, pack_back, 0)

        @pl.when(core != h)
        def _():
            send_to(chip * 2 + h, k, send_a, back, ret_sem)

        def send_half(step, carry):
            pc, pk = chip_step(step, c, k)
            send_to(pc * 2 + h, pk, send_a, back, ret_sem)
            return carry

        lax.fori_loop(1, 64, send_half, 0)
    back[pl.ds(me, 1)] = send_a[pl.ds(me, 1)]

    wait_all(rs1, rs_sem.at[1], 24)

    def line_sum(i, carry):
        own = dkb[at_b * step_b + (i // 2) * step_m + lax.rem(i, 2)].astype(F32)
        for s in range(3):
            own = own + rs1[s * 8 + i].astype(F32)
        mid[i] = own.astype(BF16)
        return carry

    lax.fori_loop(0, 8, line_sum, 0)
    lax.fori_loop(1, 8, send_mid, 0)

    def grad_in(n, carry):
        rows = pl.ds(pl.multiple_of(n * 256, 256), 256)
        out_a[rows, :] = dot_tn(xb[:, rows], gub[:, 0:768]).astype(BF16)
        out_b[rows, :] = dot_tn(xb[:, rows], gub[:, 768:1536]).astype(BF16)
        return carry

    lax.fori_loop(0, 8, grad_in, 0)
    outs = [
        pltpu.make_async_copy(src, dst, out_sem.at[i])
        for i, (src, dst) in enumerate(((out_a, gg_hbm), (out_b, gu_hbm), (out_d, gd_hbm)))
    ]
    outs[0].start()
    outs[1].start()

    def grad_out(n, carry):
        cols = pl.ds(pl.multiple_of(n * 512, 512), 512)
        out_d[:, cols] = dot_tn(hb[...], yb[:, cols]).astype(BF16)
        return carry

    lax.fori_loop(0, 4, grad_out, 0)
    outs[2].start()

    wait_all(rs1, rs_sem.at[0], 24)
    wait_all(rs2, rs_sem.at[2], 7)
    wait_all(rs2, rs_sem.at[3], 7)
    total = mid[at_m * 2 + zh].astype(F32)
    for s in range(7):
        total = total + rs2[s].astype(F32)
    for h in range(2):
        dk_ref[h * HALF : (h + 1) * HALF, :] = total[h, :, 0:128].astype(BF16)
        dv_ref[h * HALF : (h + 1) * HALF, :] = total[h, :, 128:256].astype(BF16)
    dq_copy.wait()
    dq_ref[...] = jnp.transpose((dqs[0] + dqr[...]) * score_scale).astype(BF16)

    wait_all(gt_send, gt_sem.at[0], DEVS - 1)
    wait_all(gt_recv, gt_sem.at[1], DEVS - 1)
    slot_gates = gt_recv[...].astype(F32)[:, 0, :]
    halves = []
    for h in range(2):
        acc = jnp.zeros((64, HALF), F32)
        for r in range(CAP):
            first = h * 320 + r * 64
            acc = acc + table[first : first + 64, :].astype(F32) * slot_gates[
                h * 64 : (h + 1) * 64, r : r + 1
            ]
        halves.append(acc)
    gate_grads = jnp.concatenate(halves, axis=0)
    for j in range(8):
        dgates_ref[j : j + 1, :] = (
            jnp.sum(hit(j) * gate_grads, axis=0, keepdims=True) / gates[j : j + 1, :]
        ).astype(BF16)

    wait_all(send_b, b_sem.at[0], DEVS - 1)
    wait_all(send_a, ret_sem.at[0], DEVS - 1)
    wait_all(back, ret_sem.at[1], DEVS - 1)
    unpack(back, slb)

    def combine(n, carry):
        cols = pl.ds(pl.multiple_of(n * 512, 512), 512)
        drows_ref[:, cols] = dot_tn(table[...], slb[:, cols]).astype(BF16)
        return carry

    lax.fori_loop(0, 4, combine, 0)
    for copy in outs:
        copy.wait()


def hand_over(*refs):
    small, big = refs[0:5], refs[5:8]
    small_out, big_out = refs[8:13], refs[13:16]
    held, in_sem, out_sem = refs[16:19], refs[19], refs[20]
    steps = []
    for i in range(3):
        count = 4
        depth = big[i].shape[0] // count
        for part in range(count):
            rows = pl.ds(part * depth, depth)
            sem = i * count + part
            steps.append(
                (
                    pltpu.make_async_copy(big[i].at[rows], held[i].at[rows], in_sem.at[sem]),
                    pltpu.make_async_copy(held[i].at[rows], big_out[i].at[rows], out_sem.at[sem]),
                )
            )
    for fetch, _ in steps:
        fetch.start()
    for src, dst in zip(small, small_out):
        dst[...] = src[...]
    for fetch, store in steps:
        fetch.wait()
        store.start()
    for _, store in steps:
        store.wait()


def shards(
    query_rows,
    key_rows,
    value_rows,
    attn_out,
    attn_grad,
    log_total,
    stretch_order,
    moe_rows,
    moe_grad,
    expert_ids,
    gate_prob,
    gate_weight,
    up_weight,
    down_weight,
):
    tok, heads, size = query_rows.shape
    flat = tok * heads
    rows_here, width = moe_rows.shape
    hidden = gate_weight.shape[2]
    vmem = pl.BlockSpec(memory_space=pltpu.VMEM)
    smem = pl.BlockSpec(memory_space=pltpu.SMEM)
    hbm = pl.BlockSpec(memory_space=pl.ANY)
    chunk = (DEVS, CAP, TILES, 128)
    slots = DEVS * CAP
    shapes = (
        jax.ShapeDtypeStruct((flat, size), BF16),
        jax.ShapeDtypeStruct((tok, size), BF16),
        jax.ShapeDtypeStruct((tok, size), BF16),
        jax.ShapeDtypeStruct((rows_here, width), BF16),
        jax.ShapeDtypeStruct((8, rows_here), BF16),
        jax.ShapeDtypeStruct((width, hidden), BF16),
        jax.ShapeDtypeStruct((width, hidden), BF16),
        jax.ShapeDtypeStruct((hidden, width), BF16),
    )
    results = pl.pallas_call(
        layer_kernel,
        out_shape=shapes,
        in_specs=[vmem] * 6 + [smem] + [vmem] * 4 + [hbm] * 3,
        out_specs=(vmem,) * 5 + (hbm,) * 3,
        scratch_shapes=[
            pltpu.VMEM((2, HALF, 256), BF16),
            pltpu.VMEM((CHIPS, 2, HALF, 256), BF16),
            pltpu.VMEM((CHIPS, 2, HALF, 256), BF16),
            pltpu.VMEM((24, 2, HALF, 256), BF16),
            pltpu.VMEM((8, 2, HALF, 256), BF16),
            pltpu.VMEM((7, 2, HALF, 256), BF16),
            pltpu.VMEM((slots, HALF), BF16),
            pltpu.VMEM((slots, HALF), BF16),
            pltpu.VMEM((2, flat, size), BF16),
            pltpu.VMEM((2, flat, size), BF16),
            pltpu.VMEM((2, 8, flat), F32),
            pltpu.VMEM((2, size, flat), F32),
            pltpu.VMEM((size, flat), F32),
            pltpu.VMEM((256, 256), BF16),
            pltpu.VMEM(chunk, BF16),
            pltpu.VMEM(chunk, BF16),
            pltpu.VMEM(chunk, BF16),
            pltpu.VMEM(chunk, BF16),
            pltpu.VMEM(chunk, BF16),
            pltpu.VMEM((DEVS, 16, 128), BF16),
            pltpu.VMEM((DEVS, 16, 128), BF16),
            pltpu.VMEM((slots, width), BF16),
            pltpu.VMEM((slots, width), BF16),
            pltpu.VMEM((slots, width), BF16),
            pltpu.VMEM((width, hidden), BF16),
            pltpu.VMEM((width, hidden), BF16),
            pltpu.VMEM((hidden, width), BF16),
            pltpu.VMEM((slots, hidden), F32),
            pltpu.VMEM((slots, hidden), F32),
            pltpu.VMEM((slots, 2 * hidden), BF16),
            pltpu.VMEM((slots, hidden), BF16),
            pltpu.VMEM((width, hidden), BF16),
            pltpu.VMEM((width, hidden), BF16),
            pltpu.VMEM((hidden, width), BF16),
            pltpu.SemaphoreType.DMA((3,)),
            pltpu.SemaphoreType.DMA((3,)),
            pltpu.SemaphoreType.DMA((4,)),
            pltpu.SemaphoreType.DMA((6,)),
            pltpu.SemaphoreType.DMA((2,)),
            pltpu.SemaphoreType.DMA((2,)),
            pltpu.SemaphoreType.DMA((4,)),
            pltpu.SemaphoreType.DMA((2,)),
            pltpu.SemaphoreType.DMA((2,)),
            pltpu.SemaphoreType.DMA((2,)),
        ],
        compiler_params=pltpu.CompilerParams(
            collective_id=0, has_side_effects=True, vmem_limit_bytes=62 * 1024 * 1024
        ),
    )(
        query_rows.reshape(flat, size),
        key_rows.reshape(tok, size),
        value_rows.reshape(tok, size),
        attn_out.reshape(flat, size),
        attn_grad.reshape(flat, size),
        log_total.T,
        stretch_order,
        moe_rows,
        moe_grad,
        expert_ids.T,
        gate_prob.T,
        gate_weight[0],
        up_weight[0],
        down_weight[0],
    )
    results = pl.pallas_call(
        hand_over,
        out_shape=shapes,
        in_specs=[vmem] * 5 + [hbm] * 3,
        out_specs=(vmem,) * 5 + (hbm,) * 3,
        scratch_shapes=[pltpu.VMEM(shape.shape, BF16) for shape in shapes[5:8]]
        + [pltpu.SemaphoreType.DMA((12,))] * 2,
        compiler_params=pltpu.CompilerParams(vmem_limit_bytes=60 * 1024 * 1024),
    )(*results)
    d_query, d_key, d_value, d_rows, d_gates, grad_gate, grad_up, grad_down = results
    return (
        d_query.reshape(tok, heads, size),
        d_key.reshape(tok, 1, size),
        d_value.reshape(tok, 1, size),
        d_rows,
        d_gates.T,
        grad_gate[None],
        grad_up[None],
        grad_down[None],
    )


def solution(mesh):
    both = ("ctx", "kv")
    heads = P("ctx", "kv", None)
    tokens = P(both, None)
    experts = P(both, None, None)
    return jax.shard_map(
        shards,
        mesh=mesh,
        in_specs=(heads,) * 5
        + (P("ctx", "kv"), P())
        + (tokens,) * 4
        + (experts,) * 3,
        out_specs=(heads,) * 3 + (tokens,) * 2 + (experts,) * 3,
        check_vma=False,
    )
```

```python
import functools
import math

import jax
import jax.numpy as jnp
from jax import lax
from jax.experimental import pallas as pl
from jax.experimental.pallas import tpu as pltpu
from jax.sharding import PartitionSpec as P

MESH = pl.DeviceIdType.MESH
LOG2E = 1.4426950408889634
F32 = jnp.float32
BF16 = jnp.bfloat16
CAP = 5
TILES = 16
DEVS = 128
CHIPS = 32
HALF = 64


def chip_step(step, c, k):
    s = lax.rem(step * 29, 64)
    x = lax.rem(c // 16 + lax.rem(s, 4), 4)
    s = s // 4
    y = lax.rem(lax.rem(c // 4, 4) + lax.rem(s, 4), 4)
    z = lax.rem(lax.rem(c // 2, 2) * 2 + k + s // 4, 4)
    return (x * 4 + y) * 2 + z // 2, lax.rem(z, 2)


def any_partner(step, c, k):
    chip, kk = chip_step(step // 2, c, k)
    return chip * 2 + lax.rem(lax.rem(c, 2) + lax.rem(step, 2), 2), kk


def place(c, k):
    return lax.rem(c, 2) * 64 + (c // 2) * 2 + k


def dot(a, b):
    return jnp.dot(a, b, preferred_element_type=F32)


def dot_nt(a, b):
    return lax.dot_general(a, b, (((1,), (1,)), ((), ())), preferred_element_type=F32)


def dot_tn(a, b):
    return lax.dot_general(a, b, (((0,), (0,)), ((), ())), preferred_element_type=F32)


def slot_row(block, r):
    return pl.multiple_of((block // 4) * (CAP * HALF) + r * HALF + lax.rem(block, 4) * 16, 16)


def pack_block(block, perm, flat, chunks):
    cat = jnp.concatenate(
        [
            jnp.concatenate(
                [flat[pl.ds(slot_row(block, r), 16), k * 128 : (k + 1) * 128] for k in range(TILES)],
                axis=0,
            )
            for r in range(CAP)
        ],
        axis=1,
    )
    out = dot(perm, cat).astype(BF16)
    for r in range(CAP):
        chunks[pl.ds(block * 16, 16), r] = out[:, r * 128 : (r + 1) * 128].reshape(16, TILES, 128)


def unpack_block(block, perm, chunks, flat):
    cat = jnp.concatenate(
        [chunks[pl.ds(block * 16, 16), r].reshape(256, 128) for r in range(CAP)], axis=1
    )
    out = dot(perm, cat).astype(BF16)
    for r in range(CAP):
        for k in range(TILES):
            flat[pl.ds(slot_row(block, r), 16), k * 128 : (k + 1) * 128] = out[
                k * 16 : (k + 1) * 16, r * 128 : (r + 1) * 128
            ]


def layer_kernel(
    q_ref,
    k_ref,
    v_ref,
    o_ref,
    g_ref,
    log_ref,
    order_ref,
    rows_ref,
    mgrad_ref,
    ids_ref,
    gate_ref,
    wg_hbm,
    wu_hbm,
    wd_hbm,
    dq_ref,
    dk_ref,
    dv_ref,
    drows_ref,
    dgates_ref,
    out_a,
    out_b,
    out_d,
    kv_own,
    kvb,
    dkb,
    rs1,
    mid,
    rs2,
    table,
    gtable,
    qb,
    gb,
    st,
    dqs,
    dqr,
    perm_ref,
    send_a,
    send_b,
    recv_a,
    recv_b,
    back,
    gt_send,
    gt_recv,
    xb,
    yb,
    slb,
    wg,
    wu,
    wd,
    act_g,
    act_u,
    gub,
    hb,
    w_sem,
    kv_sem,
    q_sem,
    a_sem,
    b_sem,
    rs_sem,
    dq_sem,
    ret_sem,
    gt_sem,
):
    c = lax.axis_index("ctx")
    k = lax.axis_index("kv")
    me = place(c, k)
    chip = c // 2
    core = lax.rem(c, 2)
    other = chip * 2 + 1 - core
    zh = lax.rem(chip, 2)
    at_x = chip // 8
    at_y = lax.rem(chip // 2, 4)
    at_b = at_x * (1 - core) + at_y * core
    at_m = at_y * (1 - core) + at_x * core
    step_b = 8 - 6 * core
    step_m = 2 + 6 * core
    score_scale = 1.0 / math.sqrt(128.0)

    weights = [
        pltpu.make_async_copy(src, dst, w_sem.at[i])
        for i, (src, dst) in enumerate(((wg_hbm, wg), (wu_hbm, wu), (wd_hbm, wd)))
    ]
    for copy in weights:
        copy.start()

    barrier = pltpu.get_barrier_semaphore()

    def greet(step, carry):
        pc, pk = any_partner(step, c, k)
        pl.semaphore_signal(barrier, inc=1, device_id=(pc, pk), device_id_type=MESH)
        return carry

    lax.fori_loop(1, DEVS, greet, 0)

    for h in range(2):
        kv_own[h, :, 0:128] = k_ref[h * HALF : (h + 1) * HALF, :]
        kv_own[h, :, 128:256] = v_ref[h * HALF : (h + 1) * HALF, :]
    qb[0] = q_ref[...]
    gb[0] = g_ref[...]
    prod = g_ref[...].astype(F32) * o_ref[...].astype(F32)
    hi = prod.astype(BF16)
    low = (prod - hi.astype(F32)).astype(BF16)
    ones = jnp.ones((8, 128), BF16)
    delta = dot_nt(ones, hi) + dot_nt(ones, low)
    logs = log_ref[...]
    log_hi = logs.astype(BF16)
    rest = logs - log_hi.astype(F32)
    log_mid = rest.astype(BF16)
    log_low = (rest - log_mid.astype(F32)).astype(BF16)
    spread = (
        lax.broadcasted_iota(jnp.int32, (128, 1024), 1) // 8
        == lax.broadcasted_iota(jnp.int32, (128, 1024), 0)
    ).astype(BF16)
    wide = dot(log_hi, spread) + dot(log_mid, spread) + dot(log_low, spread)
    row8 = lax.broadcasted_iota(jnp.int32, (8, 1024), 0)
    mine = row8 == lax.rem(lax.broadcasted_iota(jnp.int32, (8, 1024), 1), 8)
    log_row = jnp.sum(jnp.where(mine, wide, 0.0), axis=0, keepdims=True)
    st[0] = jnp.where(row8 == 0, log_row * LOG2E, delta)

    spot = lax.broadcasted_iota(jnp.int32, (DEVS, HALF), 0)
    expert = (lax.rem(spot, 64) // 2) * 4 + (spot // 64) * 2 + lax.rem(spot, 2)
    gates = gate_ref[...].astype(F32)

    def hit(j):
        return jnp.where(expert == ids_ref[j : j + 1, :], 1.0, 0.0)

    named = functools.reduce(jnp.add, [hit(j) for j in range(8)])
    gate_of = functools.reduce(jnp.add, [hit(j) * gates[j : j + 1, :] for j in range(8)])
    before = (
        lax.broadcasted_iota(jnp.int32, (HALF, HALF), 0)
        < lax.broadcasted_iota(jnp.int32, (HALF, HALF), 1)
    ).astype(BF16)
    rank = dot(named.astype(BF16), before)
    for r in range(CAP):
        pick = jnp.where(rank == float(r), named, 0.0)
        scaled = (pick * gate_of).astype(BF16)
        pick = pick.astype(BF16)
        for h in range(2):
            first = h * 320 + r * 64
            table[first : first + 64, :] = pick[h * 64 : (h + 1) * 64]
            gtable[first : first + 64, :] = scaled[h * 64 : (h + 1) * 64]
    ri = lax.broadcasted_iota(jnp.int32, (256, 256), 0)
    ci = lax.broadcasted_iota(jnp.int32, (256, 256), 1)
    perm_ref[...] = (
        jnp.where(ri // 16 == lax.rem(ci, 16), 1.0, 0.0)
        * jnp.where(lax.rem(ri, 16) == ci // 16, 1.0, 0.0)
    ).astype(BF16)

    def gather(values, chosen, flat, chunks):
        def cols(n, carry):
            span = pl.ds(pl.multiple_of(n * 512, 512), 512)
            flat[:, span] = dot(chosen[...], values[:, span]).astype(BF16)
            return carry

        lax.fori_loop(0, 4, cols, 0)

        def pack(block, carry):
            pack_block(block, perm_ref[...], flat, chunks)
            return carry

        lax.fori_loop(0, 8, pack, 0)

    def send_to(pc, pk, chunks, got, sems):
        pltpu.make_async_remote_copy(
            src_ref=chunks.at[place(pc, pk)],
            dst_ref=got.at[me],
            send_sem=sems.at[0],
            recv_sem=sems.at[1],
            device_id=(pc, pk),
            device_id_type=MESH,
        ).start()

    def send_all(chunks, got, sems, first=1, last=DEVS):
        def send(step, carry):
            pc, pk = any_partner(step, c, k)
            send_to(pc, pk, chunks, got, sems)
            return carry

        lax.fori_loop(first, last, send, 0)

    def wait_all(buf, sem, count):
        part = buf.at[pl.ds(0, count)]
        pltpu.make_async_copy(part, part, sem).wait()

    gather(rows_ref, table, xb, send_a)

    pl.semaphore_wait(barrier, DEVS - 1)

    to_core = [
        pltpu.make_async_remote_copy(
            src_ref=buf.at[0],
            dst_ref=buf.at[1],
            send_sem=q_sem.at[i],
            recv_sem=q_sem.at[3 + i],
            device_id=(other, k),
            device_id_type=MESH,
        )
        for i, buf in enumerate((qb, gb, st))
    ]
    for copy in to_core:
        copy.start()

    def near(step):
        return lax.rem(at_m + lax.rem(step, 4), 4), lax.rem(zh + step // 4, 2)

    def send_kv(step, carry):
        m, z = near(step)
        pltpu.make_async_remote_copy(
            src_ref=kv_own,
            dst_ref=kvb.at[chip],
            send_sem=kv_sem.at[0],
            recv_sem=kv_sem.at[1],
            device_id=((at_b * step_b + m * step_m + z) * 2 + core, k),
            device_id_type=MESH,
        ).start()
        return carry

    lax.fori_loop(1, 8, send_kv, 0)
    send_all(send_a, recv_a, a_sem, 1, 17)
    recv_a[pl.ds(me, 1)] = send_a[pl.ds(me, 1)]
    kvb[pl.ds(chip, 1)] = kv_own[...].reshape(1, 2, HALF, 256)
    wait_all(kvb, kv_sem.at[1], 7)

    def pass_kv(step, carry):
        b = lax.rem(at_b + 1 + lax.rem(step, 3), 4)
        i = step // 3
        block = at_b * step_b + (i // 2) * step_m + lax.rem(i, 2)
        pltpu.make_async_remote_copy(
            src_ref=kvb.at[block],
            dst_ref=kvb.at[block],
            send_sem=kv_sem.at[2],
            recv_sem=kv_sem.at[3],
            device_id=((b * step_b + at_m * step_m + zh) * 2 + core, k),
            device_id_type=MESH,
        ).start()
        return carry

    lax.fori_loop(0, 24, pass_kv, 0)
    send_all(send_a, recv_a, a_sem, 17, DEVS)

    gather(mgrad_ref, gtable, yb, send_b)
    send_all(send_b, recv_b, b_sem)
    recv_b[pl.ds(me, 1)] = send_b[pl.ds(me, 1)]

    for copy in to_core:
        copy.wait()
    wait_all(kvb, kv_sem.at[0], 7)
    wait_all(kvb, kv_sem.at[2], 24)
    wait_all(kvb, kv_sem.at[3], 24)
    gap = (
        lax.broadcasted_iota(jnp.int32, (HALF, 512), 0)
        - lax.broadcasted_iota(jnp.int32, (HALF, 512), 1) // 8
    )
    dqs[...] = jnp.zeros_like(dqs)

    def key_tile(i, carry):
        for late_key in range(2):
            kv = kvb[pl.ds(i * 4, 4), late_key].reshape(256, 256)
            key_part = kv[:, 0:128]
            value_part = kv[:, 128:256]
            dk_sum = jnp.zeros((256, 128), F32)
            dv_sum = jnp.zeros((256, 128), F32)
            for late_q in range(late_key, 2):
                for who in range(2):
                    span = slice(late_q * 512, (late_q + 1) * 512)
                    qs = qb[who, span, :]
                    gs = gb[who, span, :]
                    shifted = dot_nt(key_part, qs) * (score_scale * LOG2E) - st[who, 0:1, span]
                    if late_q == late_key:
                        owner = c if who == 0 else other
                        own_stretch = order_ref[2 * owner + late_q]
                        pieces = []
                        for s in range(4):
                            key_stretch = order_ref[2 * ((i * 4 + s) * 2 + core) + late_key]
                            room = (own_stretch - key_stretch) * HALF
                            pieces.append(
                                jnp.where(gap <= room, shifted[s * HALF : (s + 1) * HALF], -1e30)
                            )
                        shifted = jnp.concatenate(pieces, axis=0)
                    probs = jnp.exp2(shifted)
                    dv_sum = dv_sum + dot(probs.astype(BF16), gs)
                    d_scores = (probs * (dot_nt(value_part, gs) - st[who, 1:2, span])).astype(BF16)
                    dk_sum = dk_sum + dot(d_scores, qs)
                    dqs[who, :, span] += dot_tn(key_part, d_scores)
            both = jnp.concatenate([dk_sum * score_scale, dv_sum], axis=1).astype(BF16)
            dkb[pl.ds(i * 4, 4), late_key] = both.reshape(4, HALF, 256)
        return carry

    lax.fori_loop(0, CHIPS // 4, key_tile, 0)

    dq_copy = pltpu.make_async_remote_copy(
        src_ref=dqs.at[1],
        dst_ref=dqr,
        send_sem=dq_sem.at[0],
        recv_sem=dq_sem.at[1],
        device_id=(other, k),
        device_id_type=MESH,
    )
    dq_copy.start()

    def send_partial(step, carry):
        shift = 1 + lax.rem(step, 3)
        b = lax.rem(at_b + shift, 4)
        i = step // 3
        pltpu.make_async_remote_copy(
            src_ref=dkb.at[b * step_b + (i // 2) * step_m + lax.rem(i, 2)],
            dst_ref=rs1.at[(shift - 1) * 8 + i],
            send_sem=rs_sem.at[0],
            recv_sem=rs_sem.at[1],
            device_id=((b * step_b + at_m * step_m + zh) * 2 + core, k),
            device_id_type=MESH,
        ).start()
        return carry

    def send_mid(step, carry):
        m, z = near(step)
        pltpu.make_async_remote_copy(
            src_ref=mid.at[m * 2 + z],
            dst_ref=rs2.at[step - 1],
            send_sem=rs_sem.at[2],
            recv_sem=rs_sem.at[3],
            device_id=((at_b * step_b + m * step_m + z) * 2 + core, k),
            device_id_type=MESH,
        ).start()
        return carry

    def unpack(chunks, flat):
        def body(block, carry):
            unpack_block(block, perm_ref[...], chunks, flat)
            return carry

        lax.fori_loop(0, 8, body, 0)

    wait_all(recv_a, a_sem.at[1], DEVS - 1)
    unpack(recv_a, xb)
    weights[0].wait()
    weights[1].wait()

    def gate_up(n, carry):
        cols = pl.ds(pl.multiple_of(n * 256, 256), 256)
        act_g[:, cols] = dot(xb[...], wg[:, cols])
        act_u[:, cols] = dot(xb[...], wu[:, cols])
        return carry

    lax.fori_loop(0, 3, gate_up, 0)
    weights[2].wait()
    wait_all(send_a, a_sem.at[0], DEVS - 1)
    wait_all(recv_b, b_sem.at[1], DEVS - 1)
    lax.fori_loop(0, 24, send_partial, 0)
    unpack(recv_b, yb)

    def hidden_part(n, gate_sum):
        cols = pl.ds(pl.multiple_of(n * 256, 256), 256)
        cols_up = pl.ds(pl.multiple_of(n * 256 + 768, 256), 256)
        projected = dot_nt(yb[...], wd[cols, :])
        ga = act_g[:, cols]
        ua = act_u[:, cols]
        sig = jax.nn.sigmoid(ga)
        silu = ga * sig
        hidden = (silu * ua).astype(BF16)
        hb[:, cols] = hidden
        gub[:, cols] = (projected * ua * sig * (1.0 + ga * (1.0 - sig))).astype(BF16)
        gub[:, cols_up] = (projected * silu).astype(BF16)
        return gate_sum + jnp.sum(projected * hidden.astype(F32), axis=1, keepdims=True)

    gate_sum = lax.fori_loop(0, 3, hidden_part, jnp.zeros((640, 1), F32))
    lane_h = lax.broadcasted_iota(jnp.int32, (HALF, 128), 1)
    for h in range(2):
        tile = jnp.zeros((HALF, 128), F32)
        for r in range(CAP):
            first = h * 320 + r * 64
            tile = jnp.where(lane_h == r, gate_sum[first : first + 64], tile)
        gt_send[h * HALF : (h + 1) * HALF] = jnp.broadcast_to(
            tile[:, None, :], (HALF, 16, 128)
        ).astype(BF16)

    for h in range(2):
        span = slice(h * 320, (h + 1) * 320)

        def slot_cols(n, carry):
            cols = pl.ds(pl.multiple_of(n * 256, 256), 256)
            slb[span, cols] = (
                dot_nt(gub[span, 0:768], wg[cols, :]) + dot_nt(gub[span, 768:1536], wu[cols, :])
            ).astype(BF16)
            return carry

        lax.fori_loop(0, 8, slot_cols, 0)

        def pack_back(block, carry):
            pack_block(block, perm_ref[...], slb, send_a)
            return carry

        lax.fori_loop(h * 4, h * 4 + 4, pack_back, 0)

        @pl.when(core != h)
        def _():
            send_to(chip * 2 + h, k, send_a, back, ret_sem)

        def send_half(step, carry):
            pc, pk = chip_step(step, c, k)
            send_to(pc * 2 + h, pk, send_a, back, ret_sem)
            return carry

        lax.fori_loop(1, 64, send_half, 0)
    back[pl.ds(me, 1)] = send_a[pl.ds(me, 1)]
    send_all(gt_send, gt_recv, gt_sem)
    gt_recv[pl.ds(me, 1)] = gt_send[pl.ds(me, 1)]

    wait_all(rs1, rs_sem.at[1], 24)

    def line_sum(i, carry):
        own = dkb[at_b * step_b + (i // 2) * step_m + lax.rem(i, 2)].astype(F32)
        for s in range(3):
            own = own + rs1[s * 8 + i].astype(F32)
        mid[i] = own.astype(BF16)
        return carry

    lax.fori_loop(0, 8, line_sum, 0)
    lax.fori_loop(1, 8, send_mid, 0)

    def grad_in(n, carry):
        rows = pl.ds(pl.multiple_of(n * 256, 256), 256)
        out_a[rows, :] = dot_tn(xb[:, rows], gub[:, 0:768]).astype(BF16)
        out_b[rows, :] = dot_tn(xb[:, rows], gub[:, 768:1536]).astype(BF16)
        return carry

    lax.fori_loop(0, 8, grad_in, 0)
    def grad_out(n, carry):
        cols = pl.ds(pl.multiple_of(n * 512, 512), 512)
        out_d[:, cols] = dot_tn(hb[...], yb[:, cols]).astype(BF16)
        return carry

    lax.fori_loop(0, 4, grad_out, 0)

    wait_all(rs1, rs_sem.at[0], 24)
    wait_all(rs2, rs_sem.at[2], 7)
    wait_all(rs2, rs_sem.at[3], 7)
    total = mid[at_m * 2 + zh].astype(F32)
    for s in range(7):
        total = total + rs2[s].astype(F32)
    for h in range(2):
        dk_ref[h * HALF : (h + 1) * HALF, :] = total[h, :, 0:128].astype(BF16)
        dv_ref[h * HALF : (h + 1) * HALF, :] = total[h, :, 128:256].astype(BF16)
    dq_copy.wait()
    dq_ref[...] = jnp.transpose((dqs[0] + dqr[...]) * score_scale).astype(BF16)

    wait_all(gt_send, gt_sem.at[0], DEVS - 1)
    wait_all(gt_recv, gt_sem.at[1], DEVS - 1)
    slot_gates = gt_recv[...].astype(F32)[:, 0, :]
    halves = []
    for h in range(2):
        acc = jnp.zeros((64, HALF), F32)
        for r in range(CAP):
            first = h * 320 + r * 64
            acc = acc + table[first : first + 64, :].astype(F32) * slot_gates[
                h * 64 : (h + 1) * 64, r : r + 1
            ]
        halves.append(acc)
    gate_grads = jnp.concatenate(halves, axis=0)
    for j in range(8):
        dgates_ref[j : j + 1, :] = (
            jnp.sum(hit(j) * gate_grads, axis=0, keepdims=True) / gates[j : j + 1, :]
        ).astype(BF16)

    wait_all(send_b, b_sem.at[0], DEVS - 1)
    wait_all(send_a, ret_sem.at[0], DEVS - 1)
    wait_all(back, ret_sem.at[1], DEVS - 1)
    unpack(back, slb)

    def combine(n, carry):
        cols = pl.ds(pl.multiple_of(n * 512, 512), 512)
        drows_ref[:, cols] = dot_tn(table[...], slb[:, cols]).astype(BF16)
        return carry

    lax.fori_loop(0, 4, combine, 0)


def hand_over(*refs):
    copies = [pltpu.make_async_copy(refs[i], refs[8 + i], refs[16].at[i]) for i in range(8)]
    for copy in reversed(copies):
        copy.start()
    for copy in copies:
        copy.wait()


def shards(
    query_rows,
    key_rows,
    value_rows,
    attn_out,
    attn_grad,
    log_total,
    stretch_order,
    moe_rows,
    moe_grad,
    expert_ids,
    gate_prob,
    gate_weight,
    up_weight,
    down_weight,
):
    tok, heads, size = query_rows.shape
    flat = tok * heads
    rows_here, width = moe_rows.shape
    hidden = gate_weight.shape[2]
    vmem = pl.BlockSpec(memory_space=pltpu.VMEM)
    smem = pl.BlockSpec(memory_space=pltpu.SMEM)
    hbm = pl.BlockSpec(memory_space=pl.ANY)
    chunk = (DEVS, CAP, TILES, 128)
    slots = DEVS * CAP
    shapes = (
        jax.ShapeDtypeStruct((flat, size), BF16),
        jax.ShapeDtypeStruct((tok, size), BF16),
        jax.ShapeDtypeStruct((tok, size), BF16),
        jax.ShapeDtypeStruct((rows_here, width), BF16),
        jax.ShapeDtypeStruct((8, rows_here), BF16),
        jax.ShapeDtypeStruct((width, hidden), BF16),
        jax.ShapeDtypeStruct((width, hidden), BF16),
        jax.ShapeDtypeStruct((hidden, width), BF16),
    )
    results = pl.pallas_call(
        layer_kernel,
        out_shape=tuple(pltpu.VMEM(shape.shape, BF16) for shape in shapes),
        in_specs=[vmem] * 6 + [smem] + [vmem] * 4 + [hbm] * 3,
        out_specs=(vmem,) * 8,
        scratch_shapes=[
            pltpu.VMEM((2, HALF, 256), BF16),
            pltpu.VMEM((CHIPS, 2, HALF, 256), BF16),
            pltpu.VMEM((CHIPS, 2, HALF, 256), BF16),
            pltpu.VMEM((24, 2, HALF, 256), BF16),
            pltpu.VMEM((8, 2, HALF, 256), BF16),
            pltpu.VMEM((7, 2, HALF, 256), BF16),
            pltpu.VMEM((slots, HALF), BF16),
            pltpu.VMEM((slots, HALF), BF16),
            pltpu.VMEM((2, flat, size), BF16),
            pltpu.VMEM((2, flat, size), BF16),
            pltpu.VMEM((2, 8, flat), F32),
            pltpu.VMEM((2, size, flat), F32),
            pltpu.VMEM((size, flat), F32),
            pltpu.VMEM((256, 256), BF16),
            pltpu.VMEM(chunk, BF16),
            pltpu.VMEM(chunk, BF16),
            pltpu.VMEM(chunk, BF16),
            pltpu.VMEM(chunk, BF16),
            pltpu.VMEM(chunk, BF16),
            pltpu.VMEM((DEVS, 16, 128), BF16),
            pltpu.VMEM((DEVS, 16, 128), BF16),
            pltpu.VMEM((slots, width), BF16),
            pltpu.VMEM((slots, width), BF16),
            pltpu.VMEM((slots, width), BF16),
            pltpu.VMEM((width, hidden), BF16),
            pltpu.VMEM((width, hidden), BF16),
            pltpu.VMEM((hidden, width), BF16),
            pltpu.VMEM((slots, hidden), F32),
            pltpu.VMEM((slots, hidden), F32),
            pltpu.VMEM((slots, 2 * hidden), BF16),
            pltpu.VMEM((slots, hidden), BF16),
            pltpu.SemaphoreType.DMA((3,)),
            pltpu.SemaphoreType.DMA((4,)),
            pltpu.SemaphoreType.DMA((6,)),
            pltpu.SemaphoreType.DMA((2,)),
            pltpu.SemaphoreType.DMA((2,)),
            pltpu.SemaphoreType.DMA((4,)),
            pltpu.SemaphoreType.DMA((2,)),
            pltpu.SemaphoreType.DMA((2,)),
            pltpu.SemaphoreType.DMA((2,)),
        ],
        compiler_params=pltpu.CompilerParams(
            collective_id=0, has_side_effects=True, vmem_limit_bytes=52 * 1024 * 1024
        ),
    )(
        query_rows.reshape(flat, size),
        key_rows.reshape(tok, size),
        value_rows.reshape(tok, size),
        attn_out.reshape(flat, size),
        attn_grad.reshape(flat, size),
        log_total.T,
        stretch_order,
        moe_rows,
        moe_grad,
        expert_ids.T,
        gate_prob.T,
        gate_weight[0],
        up_weight[0],
        down_weight[0],
    )
    results = pl.pallas_call(
        hand_over,
        out_shape=shapes,
        in_specs=[hbm] * 8,
        out_specs=(hbm,) * 8,
        scratch_shapes=[pltpu.SemaphoreType.DMA((8,))],
        compiler_params=pltpu.CompilerParams(vmem_limit_bytes=16 * 1024 * 1024),
    )(*results)
    d_query, d_key, d_value, d_rows, d_gates, grad_gate, grad_up, grad_down = results
    return (
        d_query.reshape(tok, heads, size),
        d_key.reshape(tok, 1, size),
        d_value.reshape(tok, 1, size),
        d_rows,
        d_gates.T,
        grad_gate[None],
        grad_up[None],
        grad_down[None],
    )


def solution(mesh):
    both = ("ctx", "kv")
    heads = P("ctx", "kv", None)
    tokens = P(both, None)
    experts = P(both, None, None)
    return jax.shard_map(
        shards,
        mesh=mesh,
        in_specs=(heads,) * 5
        + (P("ctx", "kv"), P())
        + (tokens,) * 4
        + (experts,) * 3,
        out_specs=(heads,) * 3 + (tokens,) * 2 + (experts,) * 3,
        check_vma=False,
    )
```

```python
import functools
import math

import jax
import jax.numpy as jnp
from jax import lax
from jax.experimental import pallas as pl
from jax.experimental.pallas import tpu as pltpu
from jax.sharding import PartitionSpec as P

MESH = pl.DeviceIdType.MESH
LOG2E = 1.4426950408889634
F32 = jnp.float32
BF16 = jnp.bfloat16
CAP = 5
TILES = 16
DEVS = 128
CHIPS = 32
HALF = 64


def chip_step(step, c, k):
    s = lax.rem(step * 29, 64)
    x = lax.rem(c // 16 + lax.rem(s, 4), 4)
    s = s // 4
    y = lax.rem(lax.rem(c // 4, 4) + lax.rem(s, 4), 4)
    z = lax.rem(lax.rem(c // 2, 2) * 2 + k + s // 4, 4)
    return (x * 4 + y) * 2 + z // 2, lax.rem(z, 2)


def any_partner(step, c, k):
    chip, kk = chip_step(step // 2, c, k)
    return chip * 2 + lax.rem(lax.rem(c, 2) + lax.rem(step, 2), 2), kk


def place(c, k):
    return lax.rem(c, 2) * 64 + (c // 2) * 2 + k


def dot(a, b):
    return jnp.dot(a, b, preferred_element_type=F32)


def dot_nt(a, b):
    return lax.dot_general(a, b, (((1,), (1,)), ((), ())), preferred_element_type=F32)


def dot_tn(a, b):
    return lax.dot_general(a, b, (((0,), (0,)), ((), ())), preferred_element_type=F32)


def slot_row(block, r):
    return pl.multiple_of((block // 4) * (CAP * HALF) + r * HALF + lax.rem(block, 4) * 16, 16)


def pack_block(block, perm, flat, chunks):
    cat = jnp.concatenate(
        [
            jnp.concatenate(
                [flat[pl.ds(slot_row(block, r), 16), k * 128 : (k + 1) * 128] for k in range(TILES)],
                axis=0,
            )
            for r in range(CAP)
        ],
        axis=1,
    )
    out = dot(perm, cat).astype(BF16)
    for r in range(CAP):
        chunks[pl.ds(block * 16, 16), r] = out[:, r * 128 : (r + 1) * 128].reshape(16, TILES, 128)


def unpack_block(block, perm, chunks, flat):
    cat = jnp.concatenate(
        [chunks[pl.ds(block * 16, 16), r].reshape(256, 128) for r in range(CAP)], axis=1
    )
    out = dot(perm, cat).astype(BF16)
    for r in range(CAP):
        for k in range(TILES):
            flat[pl.ds(slot_row(block, r), 16), k * 128 : (k + 1) * 128] = out[
                k * 16 : (k + 1) * 16, r * 128 : (r + 1) * 128
            ]


def layer_kernel(
    q_ref,
    k_ref,
    v_ref,
    o_ref,
    g_ref,
    log_ref,
    order_ref,
    rows_ref,
    mgrad_ref,
    ids_ref,
    gate_ref,
    wg_hbm,
    wu_hbm,
    wd_hbm,
    dq_ref,
    dk_ref,
    dv_ref,
    drows_ref,
    dgates_ref,
    out_a,
    out_b,
    out_d,
    kv_own,
    kvb,
    dkb,
    rs1,
    mid,
    rs2,
    table,
    gtable,
    qb,
    gb,
    st,
    dqs,
    dqr,
    perm_ref,
    send_a,
    send_b,
    recv_a,
    recv_b,
    back,
    xb,
    yb,
    slb,
    wg,
    wu,
    wd,
    act_g,
    act_u,
    gub,
    hb,
    w_sem,
    kv_sem,
    q_sem,
    a_sem,
    b_sem,
    rs_sem,
    dq_sem,
    ret_sem,
):
    c = lax.axis_index("ctx")
    k = lax.axis_index("kv")
    me = place(c, k)
    chip = c // 2
    core = lax.rem(c, 2)
    other = chip * 2 + 1 - core
    zh = lax.rem(chip, 2)
    at_x = chip // 8
    at_y = lax.rem(chip // 2, 4)
    at_b = at_x * (1 - core) + at_y * core
    at_m = at_y * (1 - core) + at_x * core
    step_b = 8 - 6 * core
    step_m = 2 + 6 * core
    score_scale = 1.0 / math.sqrt(128.0)

    weights = [
        pltpu.make_async_copy(src, dst, w_sem.at[i])
        for i, (src, dst) in enumerate(((wg_hbm, wg), (wu_hbm, wu), (wd_hbm, wd)))
    ]
    for copy in weights:
        copy.start()

    barrier = pltpu.get_barrier_semaphore()

    def greet(step, carry):
        pc, pk = any_partner(step, c, k)
        pl.semaphore_signal(barrier, inc=1, device_id=(pc, pk), device_id_type=MESH)
        return carry

    lax.fori_loop(1, DEVS, greet, 0)

    for h in range(2):
        kv_own[h, :, 0:128] = k_ref[h * HALF : (h + 1) * HALF, :]
        kv_own[h, :, 128:256] = v_ref[h * HALF : (h + 1) * HALF, :]
    qb[0] = q_ref[...]
    gb[0] = g_ref[...]
    prod = g_ref[...].astype(F32) * o_ref[...].astype(F32)
    hi = prod.astype(BF16)
    low = (prod - hi.astype(F32)).astype(BF16)
    ones = jnp.ones((8, 128), BF16)
    delta = dot_nt(ones, hi) + dot_nt(ones, low)
    logs = log_ref[...]
    log_hi = logs.astype(BF16)
    rest = logs - log_hi.astype(F32)
    log_mid = rest.astype(BF16)
    log_low = (rest - log_mid.astype(F32)).astype(BF16)
    spread = (
        lax.broadcasted_iota(jnp.int32, (128, 1024), 1) // 8
        == lax.broadcasted_iota(jnp.int32, (128, 1024), 0)
    ).astype(BF16)
    wide = dot(log_hi, spread) + dot(log_mid, spread) + dot(log_low, spread)
    row8 = lax.broadcasted_iota(jnp.int32, (8, 1024), 0)
    mine = row8 == lax.rem(lax.broadcasted_iota(jnp.int32, (8, 1024), 1), 8)
    log_row = jnp.sum(jnp.where(mine, wide, 0.0), axis=0, keepdims=True)
    st[0] = jnp.where(row8 == 0, log_row * LOG2E, delta)

    spot = lax.broadcasted_iota(jnp.int32, (DEVS, HALF), 0)
    expert = (lax.rem(spot, 64) // 2) * 4 + (spot // 64) * 2 + lax.rem(spot, 2)
    gates = gate_ref[...].astype(F32)

    def hit(j):
        return jnp.where(expert == ids_ref[j : j + 1, :], 1.0, 0.0)

    named = functools.reduce(jnp.add, [hit(j) for j in range(8)])
    gate_of = functools.reduce(jnp.add, [hit(j) * gates[j : j + 1, :] for j in range(8)])
    before = (
        lax.broadcasted_iota(jnp.int32, (HALF, HALF), 0)
        < lax.broadcasted_iota(jnp.int32, (HALF, HALF), 1)
    ).astype(BF16)
    rank = dot(named.astype(BF16), before)
    for r in range(CAP):
        pick = jnp.where(rank == float(r), named, 0.0)
        scaled = (pick * gate_of).astype(BF16)
        pick = pick.astype(BF16)
        for h in range(2):
            first = h * 320 + r * 64
            table[first : first + 64, :] = pick[h * 64 : (h + 1) * 64]
            gtable[first : first + 64, :] = scaled[h * 64 : (h + 1) * 64]
    ri = lax.broadcasted_iota(jnp.int32, (256, 256), 0)
    ci = lax.broadcasted_iota(jnp.int32, (256, 256), 1)
    perm_ref[...] = (
        jnp.where(ri // 16 == lax.rem(ci, 16), 1.0, 0.0)
        * jnp.where(lax.rem(ri, 16) == ci // 16, 1.0, 0.0)
    ).astype(BF16)

    def gather(values, chosen, flat, chunks):
        def cols(n, carry):
            span = pl.ds(pl.multiple_of(n * 512, 512), 512)
            flat[:, span] = dot(chosen[...], values[:, span]).astype(BF16)
            return carry

        lax.fori_loop(0, 4, cols, 0)

        def pack(block, carry):
            pack_block(block, perm_ref[...], flat, chunks)
            return carry

        lax.fori_loop(0, 8, pack, 0)

    def send_to(pc, pk, chunks, got, sems):
        pltpu.make_async_remote_copy(
            src_ref=chunks.at[place(pc, pk), pl.ds(0, CAP)],
            dst_ref=got.at[me],
            send_sem=sems.at[0],
            recv_sem=sems.at[1],
            device_id=(pc, pk),
            device_id_type=MESH,
        ).start()

    def send_all(chunks, got, sems, first=1, last=DEVS):
        def send(step, carry):
            pc, pk = any_partner(step, c, k)
            send_to(pc, pk, chunks, got, sems)
            return carry

        lax.fori_loop(first, last, send, 0)

    def send_group(group, chunks, got, send_sem, recv_sem):
        def send(step, carry):
            chip_to, pk = chip_step(step, c, k)
            pc = chip_to * 2 + lax.rem(core + group, 2)
            pltpu.make_async_remote_copy(
                src_ref=chunks.at[place(pc, pk)],
                dst_ref=got.at[me],
                send_sem=send_sem,
                recv_sem=recv_sem,
                device_id=(pc, pk),
                device_id_type=MESH,
            ).start()
            return carry

        lax.fori_loop(1 - group, 64, send, 0)

    def wait_all(buf, sem, count):
        part = buf.at[pl.ds(0, count)]
        pltpu.make_async_copy(part, part, sem).wait()

    gather(rows_ref, table, xb, send_a)

    pl.semaphore_wait(barrier, DEVS - 1)

    to_core = [
        pltpu.make_async_remote_copy(
            src_ref=buf.at[0],
            dst_ref=buf.at[1],
            send_sem=q_sem.at[i],
            recv_sem=q_sem.at[3 + i],
            device_id=(other, k),
            device_id_type=MESH,
        )
        for i, buf in enumerate((qb, gb, st))
    ]
    for copy in to_core:
        copy.start()

    def near(step):
        return lax.rem(at_m + lax.rem(step, 4), 4), lax.rem(zh + step // 4, 2)

    def send_kv(step, carry):
        m, z = near(step)
        pltpu.make_async_remote_copy(
            src_ref=kv_own,
            dst_ref=kvb.at[chip],
            send_sem=kv_sem.at[0],
            recv_sem=kv_sem.at[1],
            device_id=((at_b * step_b + m * step_m + z) * 2 + core, k),
            device_id_type=MESH,
        ).start()
        return carry

    lax.fori_loop(1, 8, send_kv, 0)
    send_all(send_a, recv_a, a_sem, 1, 17)
    recv_a[pl.ds(me, 1)] = send_a[pl.ds(me, 1), 0:CAP]
    kvb[pl.ds(chip, 1)] = kv_own[...].reshape(1, 2, HALF, 256)
    wait_all(kvb, kv_sem.at[1], 7)

    def pass_kv(step, carry):
        b = lax.rem(at_b + 1 + lax.rem(step, 3), 4)
        i = step // 3
        block = at_b * step_b + (i // 2) * step_m + lax.rem(i, 2)
        pltpu.make_async_remote_copy(
            src_ref=kvb.at[block],
            dst_ref=kvb.at[block],
            send_sem=kv_sem.at[2],
            recv_sem=kv_sem.at[3],
            device_id=((b * step_b + at_m * step_m + zh) * 2 + core, k),
            device_id_type=MESH,
        ).start()
        return carry

    lax.fori_loop(0, 24, pass_kv, 0)
    send_all(send_a, recv_a, a_sem, 17, DEVS)

    gather(mgrad_ref, gtable, yb, send_b)
    recv_b[pl.ds(me, 1)] = send_b[pl.ds(me, 1)]
    send_group(0, send_b, recv_b, b_sem.at[0], b_sem.at[1])

    for copy in to_core:
        copy.wait()
    wait_all(kvb, kv_sem.at[0], 7)
    wait_all(kvb, kv_sem.at[2], 24)
    wait_all(kvb, kv_sem.at[3], 24)
    gap = (
        lax.broadcasted_iota(jnp.int32, (HALF, 512), 0)
        - lax.broadcasted_iota(jnp.int32, (HALF, 512), 1) // 8
    )
    dqs[...] = jnp.zeros_like(dqs)

    def key_tile(i, carry):
        for late_key in range(2):
            kv = kvb[pl.ds(i * 4, 4), late_key].reshape(256, 256)
            key_part = kv[:, 0:128]
            value_part = kv[:, 128:256]
            dk_sum = jnp.zeros((256, 128), F32)
            dv_sum = jnp.zeros((256, 128), F32)
            for late_q in range(late_key, 2):
                for who in range(2):
                    span = slice(late_q * 512, (late_q + 1) * 512)
                    qs = qb[who, span, :]
                    gs = gb[who, span, :]
                    shifted = dot_nt(key_part, qs) * (score_scale * LOG2E) - st[who, 0:1, span]
                    if late_q == late_key:
                        owner = c if who == 0 else other
                        own_stretch = order_ref[2 * owner + late_q]
                        pieces = []
                        for s in range(4):
                            key_stretch = order_ref[2 * ((i * 4 + s) * 2 + core) + late_key]
                            room = (own_stretch - key_stretch) * HALF
                            pieces.append(
                                jnp.where(gap <= room, shifted[s * HALF : (s + 1) * HALF], -1e30)
                            )
                        shifted = jnp.concatenate(pieces, axis=0)
                    probs = jnp.exp2(shifted)
                    dv_sum = dv_sum + dot(probs.astype(BF16), gs)
                    d_scores = (probs * (dot_nt(value_part, gs) - st[who, 1:2, span])).astype(BF16)
                    dk_sum = dk_sum + dot(d_scores, qs)
                    dqs[who, :, span] += dot_tn(key_part, d_scores)
            both = jnp.concatenate([dk_sum * score_scale, dv_sum], axis=1).astype(BF16)
            dkb[pl.ds(i * 4, 4), late_key] = both.reshape(4, HALF, 256)
        return carry

    lax.fori_loop(0, 5, key_tile, 0)
    send_group(1, send_b, recv_b, b_sem.at[0], b_sem.at[2])
    lax.fori_loop(5, CHIPS // 4, key_tile, 0)

    dq_copy = pltpu.make_async_remote_copy(
        src_ref=dqs.at[1],
        dst_ref=dqr,
        send_sem=dq_sem.at[0],
        recv_sem=dq_sem.at[1],
        device_id=(other, k),
        device_id_type=MESH,
    )
    dq_copy.start()

    def send_partial(step, carry):
        shift = 1 + lax.rem(step, 3)
        b = lax.rem(at_b + shift, 4)
        i = step // 3
        pltpu.make_async_remote_copy(
            src_ref=dkb.at[b * step_b + (i // 2) * step_m + lax.rem(i, 2)],
            dst_ref=rs1.at[(shift - 1) * 8 + i],
            send_sem=rs_sem.at[0],
            recv_sem=rs_sem.at[1],
            device_id=((b * step_b + at_m * step_m + zh) * 2 + core, k),
            device_id_type=MESH,
        ).start()
        return carry

    def send_mid(step, carry):
        m, z = near(step)
        pltpu.make_async_remote_copy(
            src_ref=mid.at[m * 2 + z],
            dst_ref=rs2.at[step - 1],
            send_sem=rs_sem.at[2],
            recv_sem=rs_sem.at[3],
            device_id=((at_b * step_b + m * step_m + z) * 2 + core, k),
            device_id_type=MESH,
        ).start()
        return carry

    def unpack(chunks, flat, first, last):
        def body(block, carry):
            unpack_block(block, perm_ref[...], chunks, flat)
            return carry

        lax.fori_loop(first, last, body, 0)

    wait_all(recv_a, a_sem.at[1], DEVS - 1)
    unpack(recv_a, xb, 0, 8)
    weights[0].wait()
    weights[1].wait()

    def gate_up(n, carry):
        cols = pl.ds(pl.multiple_of(n * 256, 256), 256)
        act_g[:, cols] = dot(xb[...], wg[:, cols])
        act_u[:, cols] = dot(xb[...], wu[:, cols])
        return carry

    lax.fori_loop(0, 3, gate_up, 0)
    weights[2].wait()
    dq_copy.wait()
    dq_ref[...] = jnp.transpose((dqs[0] + dqr[...]) * score_scale).astype(BF16)
    wait_all(recv_a, a_sem.at[0], DEVS - 1)

    for group in range(2):
        half = lax.rem(core + group, 2)
        span = pl.ds(pl.multiple_of(half * 320, 64), 320)
        wait_all(recv_b, b_sem.at[1 + group], 63 + group)
        if group == 0:
            lax.fori_loop(0, 24, send_partial, 0)
        unpack(recv_b, yb, half * 4, half * 4 + 4)

        def hidden_part(n, gate_sum):
            cols = pl.ds(pl.multiple_of(n * 256, 256), 256)
            cols_up = pl.ds(pl.multiple_of(n * 256 + 768, 256), 256)
            projected = dot_nt(yb[span, :], wd[cols, :])
            ga = act_g[span, cols]
            ua = act_u[span, cols]
            sig = jax.nn.sigmoid(ga)
            silu = ga * sig
            hidden = (silu * ua).astype(BF16)
            hb[span, cols] = hidden
            gub[span, cols] = (projected * ua * sig * (1.0 + ga * (1.0 - sig))).astype(BF16)
            gub[span, cols_up] = (projected * silu).astype(BF16)
            return gate_sum + jnp.sum(projected * hidden.astype(F32), axis=1, keepdims=True)

        gate_sum = lax.fori_loop(0, 3, hidden_part, jnp.zeros((320, 1), F32))

        def slot_cols(n, carry):
            cols = pl.ds(pl.multiple_of(n * 256, 256), 256)
            slb[span, cols] = (
                dot_nt(gub[span, 0:768], wg[cols, :]) + dot_nt(gub[span, 768:1536], wu[cols, :])
            ).astype(BF16)
            return carry

        lax.fori_loop(0, 8, slot_cols, 0)

        def pack_back(block, carry):
            pack_block(block, perm_ref[...], slb, send_a)
            return carry

        lax.fori_loop(half * 4, half * 4 + 4, pack_back, 0)
        lane_h = lax.broadcasted_iota(jnp.int32, (HALF, 128), 1)
        tile = jnp.zeros((HALF, 128), F32)
        for r in range(CAP):
            tile = jnp.where(lane_h == r, gate_sum[r * 64 : r * 64 + 64], tile)
        send_a[pl.ds(pl.multiple_of(half * HALF, HALF), HALF), CAP] = jnp.broadcast_to(
            tile[:, None, :], (HALF, 16, 128)
        ).astype(BF16)
        send_group(group, send_a, back, ret_sem.at[0], ret_sem.at[1 + group])

        if group == 0:
            back[pl.ds(me, 1)] = send_a[pl.ds(me, 1)]

    wait_all(rs1, rs_sem.at[1], 24)

    def line_sum(i, carry):
        own = dkb[at_b * step_b + (i // 2) * step_m + lax.rem(i, 2)].astype(F32)
        for s in range(3):
            own = own + rs1[s * 8 + i].astype(F32)
        mid[i] = own.astype(BF16)
        return carry

    lax.fori_loop(0, 8, line_sum, 0)
    lax.fori_loop(1, 8, send_mid, 0)

    def grad_in(n, carry):
        rows = pl.ds(pl.multiple_of(n * 256, 256), 256)
        out_a[rows, :] = dot_tn(xb[:, rows], gub[:, 0:768]).astype(BF16)
        out_b[rows, :] = dot_tn(xb[:, rows], gub[:, 768:1536]).astype(BF16)
        return carry

    lax.fori_loop(0, 8, grad_in, 0)
    def grad_out(n, carry):
        cols = pl.ds(pl.multiple_of(n * 512, 512), 512)
        out_d[:, cols] = dot_tn(hb[...], yb[:, cols]).astype(BF16)
        return carry

    lax.fori_loop(0, 4, grad_out, 0)

    wait_all(rs1, rs_sem.at[0], 24)
    wait_all(rs2, rs_sem.at[2], 7)
    wait_all(rs2, rs_sem.at[3], 7)
    total = mid[at_m * 2 + zh].astype(F32)
    for s in range(7):
        total = total + rs2[s].astype(F32)
    for h in range(2):
        dk_ref[h * HALF : (h + 1) * HALF, :] = total[h, :, 0:128].astype(BF16)
        dv_ref[h * HALF : (h + 1) * HALF, :] = total[h, :, 128:256].astype(BF16)

    wait_all(send_b, b_sem.at[0], DEVS - 1)
    wait_all(send_a, ret_sem.at[0], DEVS - 1)
    near_spot = lax.broadcasted_iota(jnp.int32, (HALF, HALF), 0)
    gate_rows = [jnp.zeros((1, HALF), F32)] * 8
    for group in range(2):
        half = lax.rem(core + group, 2)
        wait_all(back, ret_sem.at[1 + group], 63 + group)
        unpack(back, slb, half * 4, half * 4 + 4)
        slot_gates = back[pl.ds(half * HALF, HALF), CAP].astype(F32)[:, 0, :]
        acc = jnp.zeros((HALF, HALF), F32)
        for r in range(CAP):
            first = pl.multiple_of(half * 320 + r * 64, 64)
            acc = acc + table[pl.ds(first, 64), :].astype(F32) * slot_gates[:, r : r + 1]
        owner = (near_spot // 2) * 4 + half * 2 + lax.rem(near_spot, 2)
        for j in range(8):
            named_here = owner == ids_ref[j : j + 1, :]
            gate_rows[j] = gate_rows[j] + jnp.sum(
                jnp.where(named_here, acc, 0.0), axis=0, keepdims=True
            )
    for j in range(8):
        dgates_ref[j : j + 1, :] = (gate_rows[j] / gates[j : j + 1, :]).astype(BF16)

    def combine(n, carry):
        cols = pl.ds(pl.multiple_of(n * 512, 512), 512)
        drows_ref[:, cols] = dot_tn(table[...], slb[:, cols]).astype(BF16)
        return carry

    lax.fori_loop(0, 4, combine, 0)


def hand_over(*refs):
    copies = [pltpu.make_async_copy(refs[i], refs[8 + i], refs[16].at[i]) for i in range(8)]
    for copy in reversed(copies):
        copy.start()
    for copy in copies:
        copy.wait()


def shards(
    query_rows,
    key_rows,
    value_rows,
    attn_out,
    attn_grad,
    log_total,
    stretch_order,
    moe_rows,
    moe_grad,
    expert_ids,
    gate_prob,
    gate_weight,
    up_weight,
    down_weight,
):
    tok, heads, size = query_rows.shape
    flat = tok * heads
    rows_here, width = moe_rows.shape
    hidden = gate_weight.shape[2]
    vmem = pl.BlockSpec(memory_space=pltpu.VMEM)
    smem = pl.BlockSpec(memory_space=pltpu.SMEM)
    hbm = pl.BlockSpec(memory_space=pl.ANY)
    chunk = (DEVS, CAP, TILES, 128)
    chunk_and_gates = (DEVS, CAP + 1, TILES, 128)
    slots = DEVS * CAP
    shapes = (
        jax.ShapeDtypeStruct((flat, size), BF16),
        jax.ShapeDtypeStruct((tok, size), BF16),
        jax.ShapeDtypeStruct((tok, size), BF16),
        jax.ShapeDtypeStruct((rows_here, width), BF16),
        jax.ShapeDtypeStruct((8, rows_here), BF16),
        jax.ShapeDtypeStruct((width, hidden), BF16),
        jax.ShapeDtypeStruct((width, hidden), BF16),
        jax.ShapeDtypeStruct((hidden, width), BF16),
    )
    results = pl.pallas_call(
        layer_kernel,
        out_shape=tuple(pltpu.VMEM(shape.shape, BF16) for shape in shapes),
        in_specs=[vmem] * 6 + [smem] + [vmem] * 4 + [hbm] * 3,
        out_specs=(vmem,) * 8,
        scratch_shapes=[
            pltpu.VMEM((2, HALF, 256), BF16),
            pltpu.VMEM((CHIPS, 2, HALF, 256), BF16),
            pltpu.VMEM((CHIPS, 2, HALF, 256), BF16),
            pltpu.VMEM((24, 2, HALF, 256), BF16),
            pltpu.VMEM((8, 2, HALF, 256), BF16),
            pltpu.VMEM((7, 2, HALF, 256), BF16),
            pltpu.VMEM((slots, HALF), BF16),
            pltpu.VMEM((slots, HALF), BF16),
            pltpu.VMEM((2, flat, size), BF16),
            pltpu.VMEM((2, flat, size), BF16),
            pltpu.VMEM((2, 8, flat), F32),
            pltpu.VMEM((2, size, flat), F32),
            pltpu.VMEM((size, flat), F32),
            pltpu.VMEM((256, 256), BF16),
            pltpu.VMEM(chunk_and_gates, BF16),
            pltpu.VMEM(chunk, BF16),
            pltpu.VMEM(chunk, BF16),
            pltpu.VMEM(chunk, BF16),
            pltpu.VMEM(chunk_and_gates, BF16),
            pltpu.VMEM((slots, width), BF16),
            pltpu.VMEM((slots, width), BF16),
            pltpu.VMEM((slots, width), BF16),
            pltpu.VMEM((width, hidden), BF16),
            pltpu.VMEM((width, hidden), BF16),
            pltpu.VMEM((hidden, width), BF16),
            pltpu.VMEM((slots, hidden), F32),
            pltpu.VMEM((slots, hidden), F32),
            pltpu.VMEM((slots, 2 * hidden), BF16),
            pltpu.VMEM((slots, hidden), BF16),
            pltpu.SemaphoreType.DMA((3,)),
            pltpu.SemaphoreType.DMA((4,)),
            pltpu.SemaphoreType.DMA((6,)),
            pltpu.SemaphoreType.DMA((2,)),
            pltpu.SemaphoreType.DMA((3,)),
            pltpu.SemaphoreType.DMA((4,)),
            pltpu.SemaphoreType.DMA((2,)),
            pltpu.SemaphoreType.DMA((3,)),
        ],
        compiler_params=pltpu.CompilerParams(
            collective_id=0, has_side_effects=True, vmem_limit_bytes=52 * 1024 * 1024
        ),
    )(
        query_rows.reshape(flat, size),
        key_rows.reshape(tok, size),
        value_rows.reshape(tok, size),
        attn_out.reshape(flat, size),
        attn_grad.reshape(flat, size),
        log_total.T,
        stretch_order,
        moe_rows,
        moe_grad,
        expert_ids.T,
        gate_prob.T,
        gate_weight[0],
        up_weight[0],
        down_weight[0],
    )
    results = pl.pallas_call(
        hand_over,
        out_shape=shapes,
        in_specs=[hbm] * 8,
        out_specs=(hbm,) * 8,
        scratch_shapes=[pltpu.SemaphoreType.DMA((8,))],
        compiler_params=pltpu.CompilerParams(vmem_limit_bytes=16 * 1024 * 1024),
    )(*results)
    d_query, d_key, d_value, d_rows, d_gates, grad_gate, grad_up, grad_down = results
    return (
        d_query.reshape(tok, heads, size),
        d_key.reshape(tok, 1, size),
        d_value.reshape(tok, 1, size),
        d_rows,
        d_gates.T,
        grad_gate[None],
        grad_up[None],
        grad_down[None],
    )


def solution(mesh):
    both = ("ctx", "kv")
    heads = P("ctx", "kv", None)
    tokens = P(both, None)
    experts = P(both, None, None)
    return jax.shard_map(
        shards,
        mesh=mesh,
        in_specs=(heads,) * 5
        + (P("ctx", "kv"), P())
        + (tokens,) * 4
        + (experts,) * 3,
        out_specs=(heads,) * 3 + (tokens,) * 2 + (experts,) * 3,
        check_vma=False,
    )
```

```python
import functools
import math

import jax
import jax.numpy as jnp
from jax import lax
from jax.experimental import pallas as pl
from jax.experimental.pallas import tpu as pltpu
from jax.sharding import PartitionSpec as P

MESH = pl.DeviceIdType.MESH
LOG2E = 1.4426950408889634
F32 = jnp.float32
BF16 = jnp.bfloat16
CAP = 5
TILES = 16
DEVS = 128
CHIPS = 32
HALF = 64


def chip_step(step, c, k):
    s = lax.rem(step * 29, 64)
    x = lax.rem(c // 16 + lax.rem(s, 4), 4)
    s = s // 4
    y = lax.rem(lax.rem(c // 4, 4) + lax.rem(s, 4), 4)
    z = lax.rem(lax.rem(c // 2, 2) * 2 + k + s // 4, 4)
    return (x * 4 + y) * 2 + z // 2, lax.rem(z, 2)


def any_partner(step, c, k):
    chip, kk = chip_step(step // 2, c, k)
    return chip * 2 + lax.rem(lax.rem(c, 2) + lax.rem(step, 2), 2), kk


def place(c, k):
    return lax.rem(c, 2) * 64 + (c // 2) * 2 + k


def dot(a, b):
    return jnp.dot(a, b, preferred_element_type=F32)


def dot_nt(a, b):
    return lax.dot_general(a, b, (((1,), (1,)), ((), ())), preferred_element_type=F32)


def dot_tn(a, b):
    return lax.dot_general(a, b, (((0,), (0,)), ((), ())), preferred_element_type=F32)


def slot_row(block, r):
    return pl.multiple_of((block // 4) * (CAP * HALF) + r * HALF + lax.rem(block, 4) * 16, 16)


def pack_block(block, perm, flat, chunks):
    cat = jnp.concatenate(
        [
            jnp.concatenate(
                [flat[pl.ds(slot_row(block, r), 16), k * 128 : (k + 1) * 128] for k in range(TILES)],
                axis=0,
            )
            for r in range(CAP)
        ],
        axis=1,
    )
    out = dot(perm, cat).astype(BF16)
    for r in range(CAP):
        chunks[pl.ds(block * 16, 16), r] = out[:, r * 128 : (r + 1) * 128].reshape(16, TILES, 128)


def unpack_block(block, perm, chunks, flat):
    cat = jnp.concatenate(
        [chunks[pl.ds(block * 16, 16), r].reshape(256, 128) for r in range(CAP)], axis=1
    )
    out = dot(perm, cat).astype(BF16)
    for r in range(CAP):
        for k in range(TILES):
            flat[pl.ds(slot_row(block, r), 16), k * 128 : (k + 1) * 128] = out[
                k * 16 : (k + 1) * 16, r * 128 : (r + 1) * 128
            ]


def layer_kernel(
    q_ref,
    k_ref,
    v_ref,
    o_ref,
    g_ref,
    log_ref,
    order_ref,
    rows_ref,
    mgrad_ref,
    ids_ref,
    gate_ref,
    wg_hbm,
    wu_hbm,
    wd_hbm,
    dq_ref,
    dk_ref,
    dv_ref,
    drows_ref,
    dgates_ref,
    out_a,
    out_b,
    out_d,
    kv_own,
    kvb,
    dkb,
    rs1,
    mid,
    rs2,
    table,
    gtable,
    qb,
    gb,
    st,
    dqs,
    dqr,
    perm_ref,
    send_a,
    send_b,
    recv_a,
    recv_b,
    back,
    xb,
    yb,
    slb,
    wg,
    wu,
    wd,
    act_g,
    act_u,
    gub,
    hb,
    w_sem,
    kv_sem,
    q_sem,
    a_sem,
    b_sem,
    rs_sem,
    dq_sem,
    ret_sem,
):
    c = lax.axis_index("ctx")
    k = lax.axis_index("kv")
    me = place(c, k)
    chip = c // 2
    core = lax.rem(c, 2)
    other = chip * 2 + 1 - core
    zh = lax.rem(chip, 2)
    at_x = chip // 8
    at_y = lax.rem(chip // 2, 4)
    at_b = at_x * (1 - core) + at_y * core
    at_m = at_y * (1 - core) + at_x * core
    step_b = 8 - 6 * core
    step_m = 2 + 6 * core
    score_scale = 1.0 / math.sqrt(128.0)

    weights = [
        pltpu.make_async_copy(src, dst, w_sem.at[i])
        for i, (src, dst) in enumerate(((wg_hbm, wg), (wu_hbm, wu), (wd_hbm, wd)))
    ]
    for copy in weights:
        copy.start()

    barrier = pltpu.get_barrier_semaphore()

    def greet(step, carry):
        pc, pk = any_partner(step, c, k)
        pl.semaphore_signal(barrier, inc=1, device_id=(pc, pk), device_id_type=MESH)
        return carry

    lax.fori_loop(1, DEVS, greet, 0)

    for h in range(2):
        kv_own[h, :, 0:128] = k_ref[h * HALF : (h + 1) * HALF, :]
        kv_own[h, :, 128:256] = v_ref[h * HALF : (h + 1) * HALF, :]
    qb[0] = q_ref[...]
    gb[0] = g_ref[...]
    prod = g_ref[...].astype(F32) * o_ref[...].astype(F32)
    hi = prod.astype(BF16)
    low = (prod - hi.astype(F32)).astype(BF16)
    ones = jnp.ones((8, 128), BF16)
    delta = dot_nt(ones, hi) + dot_nt(ones, low)
    logs = log_ref[...]
    log_hi = logs.astype(BF16)
    rest = logs - log_hi.astype(F32)
    log_mid = rest.astype(BF16)
    log_low = (rest - log_mid.astype(F32)).astype(BF16)
    spread = (
        lax.broadcasted_iota(jnp.int32, (128, 1024), 1) // 8
        == lax.broadcasted_iota(jnp.int32, (128, 1024), 0)
    ).astype(BF16)
    wide = dot(log_hi, spread) + dot(log_mid, spread) + dot(log_low, spread)
    row8 = lax.broadcasted_iota(jnp.int32, (8, 1024), 0)
    mine = row8 == lax.rem(lax.broadcasted_iota(jnp.int32, (8, 1024), 1), 8)
    log_row = jnp.sum(jnp.where(mine, wide, 0.0), axis=0, keepdims=True)
    st[0] = jnp.where(row8 == 0, log_row * LOG2E, delta)

    spot = lax.broadcasted_iota(jnp.int32, (DEVS, HALF), 0)
    expert = (lax.rem(spot, 64) // 2) * 4 + (spot // 64) * 2 + lax.rem(spot, 2)
    gates = gate_ref[...].astype(F32)

    def hit(j):
        return jnp.where(expert == ids_ref[j : j + 1, :], 1.0, 0.0)

    named = functools.reduce(jnp.add, [hit(j) for j in range(8)])
    gate_of = functools.reduce(jnp.add, [hit(j) * gates[j : j + 1, :] for j in range(8)])
    before = (
        lax.broadcasted_iota(jnp.int32, (HALF, HALF), 0)
        < lax.broadcasted_iota(jnp.int32, (HALF, HALF), 1)
    ).astype(BF16)
    rank = dot(named.astype(BF16), before)
    for r in range(CAP):
        pick = jnp.where(rank == float(r), named, 0.0)
        scaled = (pick * gate_of).astype(BF16)
        pick = pick.astype(BF16)
        for h in range(2):
            first = h * 320 + r * 64
            table[first : first + 64, :] = pick[h * 64 : (h + 1) * 64]
            gtable[first : first + 64, :] = scaled[h * 64 : (h + 1) * 64]
    ri = lax.broadcasted_iota(jnp.int32, (256, 256), 0)
    ci = lax.broadcasted_iota(jnp.int32, (256, 256), 1)
    perm_ref[...] = (
        jnp.where(ri // 16 == lax.rem(ci, 16), 1.0, 0.0)
        * jnp.where(lax.rem(ri, 16) == ci // 16, 1.0, 0.0)
    ).astype(BF16)

    def gather(values, chosen, flat, chunks):
        def cols(n, carry):
            span = pl.ds(pl.multiple_of(n * 512, 512), 512)
            flat[:, span] = dot(chosen[...], values[:, span]).astype(BF16)
            return carry

        lax.fori_loop(0, 4, cols, 0)

        def pack(block, carry):
            pack_block(block, perm_ref[...], flat, chunks)
            return carry

        lax.fori_loop(0, 8, pack, 0)

    def send_to(pc, pk, chunks, got, sems):
        pltpu.make_async_remote_copy(
            src_ref=chunks.at[place(pc, pk), pl.ds(0, CAP)],
            dst_ref=got.at[me],
            send_sem=sems.at[0],
            recv_sem=sems.at[1],
            device_id=(pc, pk),
            device_id_type=MESH,
        ).start()

    def send_all(chunks, got, sems, first=1, last=DEVS):
        def send(step, carry):
            pc, pk = any_partner(step, c, k)
            send_to(pc, pk, chunks, got, sems)
            return carry

        lax.fori_loop(first, last, send, 0)

    def send_group(group, chunks, got, send_sem, recv_sem):
        def send(step, carry):
            chip_to, pk = chip_step(step, c, k)
            pc = chip_to * 2 + lax.rem(core + group, 2)
            pltpu.make_async_remote_copy(
                src_ref=chunks.at[place(pc, pk)],
                dst_ref=got.at[me],
                send_sem=send_sem,
                recv_sem=recv_sem,
                device_id=(pc, pk),
                device_id_type=MESH,
            ).start()
            return carry

        lax.fori_loop(1 - group, 64, send, 0)

    def wait_all(buf, sem, count):
        part = buf.at[pl.ds(0, count)]
        pltpu.make_async_copy(part, part, sem).wait()

    gather(rows_ref, table, xb, send_a)

    pl.semaphore_wait(barrier, DEVS - 1)

    to_core = [
        pltpu.make_async_remote_copy(
            src_ref=buf.at[0],
            dst_ref=buf.at[1],
            send_sem=q_sem.at[i],
            recv_sem=q_sem.at[3 + i],
            device_id=(other, k),
            device_id_type=MESH,
        )
        for i, buf in enumerate((qb, gb, st))
    ]
    for copy in to_core:
        copy.start()

    def near(step):
        return lax.rem(at_m + lax.rem(step, 4), 4), lax.rem(zh + step // 4, 2)

    def send_kv(step, carry):
        m, z = near(step)
        pltpu.make_async_remote_copy(
            src_ref=kv_own,
            dst_ref=kvb.at[chip],
            send_sem=kv_sem.at[0],
            recv_sem=kv_sem.at[1],
            device_id=((at_b * step_b + m * step_m + z) * 2 + core, k),
            device_id_type=MESH,
        ).start()
        return carry

    lax.fori_loop(1, 8, send_kv, 0)
    send_all(send_a, recv_a, a_sem, 1, 17)
    recv_a[pl.ds(me, 1)] = send_a[pl.ds(me, 1), 0:CAP]
    kvb[pl.ds(chip, 1)] = kv_own[...].reshape(1, 2, HALF, 256)
    wait_all(kvb, kv_sem.at[1], 7)

    def pass_kv(step, carry):
        b = lax.rem(at_b + 1 + lax.rem(step, 3), 4)
        i = step // 3
        block = at_b * step_b + (i // 2) * step_m + lax.rem(i, 2)
        pltpu.make_async_remote_copy(
            src_ref=kvb.at[block],
            dst_ref=kvb.at[block],
            send_sem=kv_sem.at[2],
            recv_sem=kv_sem.at[3],
            device_id=((b * step_b + at_m * step_m + zh) * 2 + core, k),
            device_id_type=MESH,
        ).start()
        return carry

    lax.fori_loop(0, 24, pass_kv, 0)
    send_all(send_a, recv_a, a_sem, 17, DEVS)

    gather(mgrad_ref, gtable, yb, send_b)
    recv_b[pl.ds(me, 1)] = send_b[pl.ds(me, 1)]
    send_group(0, send_b, recv_b, b_sem.at[0], b_sem.at[1])

    for copy in to_core:
        copy.wait()
    wait_all(kvb, kv_sem.at[0], 7)
    wait_all(kvb, kv_sem.at[2], 24)
    wait_all(kvb, kv_sem.at[3], 24)
    gap = (
        lax.broadcasted_iota(jnp.int32, (HALF, 512), 0)
        - lax.broadcasted_iota(jnp.int32, (HALF, 512), 1) // 8
    )
    dqs[...] = jnp.zeros_like(dqs)

    def key_tile(i, carry):
        for late_key in range(2):
            kv = kvb[pl.ds(i * 4, 4), late_key].reshape(256, 256)
            key_part = kv[:, 0:128]
            value_part = kv[:, 128:256]
            dk_sum = jnp.zeros((256, 128), F32)
            dv_sum = jnp.zeros((256, 128), F32)
            for late_q in range(late_key, 2):
                for who in range(2):
                    span = slice(late_q * 512, (late_q + 1) * 512)
                    qs = qb[who, span, :]
                    gs = gb[who, span, :]
                    shifted = dot_nt(key_part, qs) * (score_scale * LOG2E) - st[who, 0:1, span]
                    if late_q == late_key:
                        owner = c if who == 0 else other
                        own_stretch = order_ref[2 * owner + late_q]
                        pieces = []
                        for s in range(4):
                            key_stretch = order_ref[2 * ((i * 4 + s) * 2 + core) + late_key]
                            room = (own_stretch - key_stretch) * HALF
                            pieces.append(
                                jnp.where(gap <= room, shifted[s * HALF : (s + 1) * HALF], -1e30)
                            )
                        shifted = jnp.concatenate(pieces, axis=0)
                    probs = jnp.exp2(shifted)
                    dv_sum = dv_sum + dot(probs.astype(BF16), gs)
                    d_scores = (probs * (dot_nt(value_part, gs) - st[who, 1:2, span])).astype(BF16)
                    dk_sum = dk_sum + dot(d_scores, qs)
                    dqs[who, :, span] += dot_tn(key_part, d_scores)
            both = jnp.concatenate([dk_sum * score_scale, dv_sum], axis=1).astype(BF16)
            dkb[pl.ds(i * 4, 4), late_key] = both.reshape(4, HALF, 256)
        return carry

    lax.fori_loop(0, 5, key_tile, 0)
    send_group(1, send_b, recv_b, b_sem.at[0], b_sem.at[2])
    lax.fori_loop(5, CHIPS // 4, key_tile, 0)

    dq_copy = pltpu.make_async_remote_copy(
        src_ref=dqs.at[1],
        dst_ref=dqr,
        send_sem=dq_sem.at[0],
        recv_sem=dq_sem.at[1],
        device_id=(other, k),
        device_id_type=MESH,
    )
    dq_copy.start()

    def send_partial(step, carry):
        shift = 1 + lax.rem(step, 3)
        b = lax.rem(at_b + shift, 4)
        i = step // 3
        pltpu.make_async_remote_copy(
            src_ref=dkb.at[b * step_b + (i // 2) * step_m + lax.rem(i, 2)],
            dst_ref=rs1.at[(shift - 1) * 8 + i],
            send_sem=rs_sem.at[0],
            recv_sem=rs_sem.at[1],
            device_id=((b * step_b + at_m * step_m + zh) * 2 + core, k),
            device_id_type=MESH,
        ).start()
        return carry

    def send_mid(step, carry):
        m, z = near(step)
        pltpu.make_async_remote_copy(
            src_ref=mid.at[m * 2 + z],
            dst_ref=rs2.at[step - 1],
            send_sem=rs_sem.at[2],
            recv_sem=rs_sem.at[3],
            device_id=((at_b * step_b + m * step_m + z) * 2 + core, k),
            device_id_type=MESH,
        ).start()
        return carry

    def unpack(chunks, flat, first, last):
        def body(block, carry):
            unpack_block(block, perm_ref[...], chunks, flat)
            return carry

        lax.fori_loop(first, last, body, 0)

    wait_all(recv_a, a_sem.at[1], DEVS - 1)
    unpack(recv_a, xb, 0, 8)
    weights[0].wait()
    weights[1].wait()

    def gate_up(n, carry):
        cols = pl.ds(pl.multiple_of(n * 256, 256), 256)
        act_g[:, cols] = dot(xb[...], wg[:, cols])
        act_u[:, cols] = dot(xb[...], wu[:, cols])
        return carry

    lax.fori_loop(0, 3, gate_up, 0)
    weights[2].wait()
    dq_copy.wait()
    dq_ref[...] = jnp.transpose((dqs[0] + dqr[...]) * score_scale).astype(BF16)
    wait_all(recv_a, a_sem.at[0], DEVS - 1)

    def line_sum(i, carry):
        own = dkb[at_b * step_b + (i // 2) * step_m + lax.rem(i, 2)].astype(F32)
        for s in range(3):
            own = own + rs1[s * 8 + i].astype(F32)
        mid[i] = own.astype(BF16)
        return carry

    for group in range(2):
        half = lax.rem(core + group, 2)
        span = pl.ds(pl.multiple_of(half * 320, 64), 320)
        if group == 1:
            wait_all(rs1, rs_sem.at[1], 24)
            lax.fori_loop(0, 8, line_sum, 0)
            lax.fori_loop(1, 8, send_mid, 0)
        wait_all(recv_b, b_sem.at[1 + group], 63 + group)
        if group == 0:
            lax.fori_loop(0, 24, send_partial, 0)
        unpack(recv_b, yb, half * 4, half * 4 + 4)

        def hidden_part(n, gate_sum):
            cols = pl.ds(pl.multiple_of(n * 256, 256), 256)
            cols_up = pl.ds(pl.multiple_of(n * 256 + 768, 256), 256)
            projected = dot_nt(yb[span, :], wd[cols, :])
            ga = act_g[span, cols]
            ua = act_u[span, cols]
            sig = jax.nn.sigmoid(ga)
            silu = ga * sig
            hidden = (silu * ua).astype(BF16)
            hb[span, cols] = hidden
            gub[span, cols] = (projected * ua * sig * (1.0 + ga * (1.0 - sig))).astype(BF16)
            gub[span, cols_up] = (projected * silu).astype(BF16)
            return gate_sum + jnp.sum(projected * hidden.astype(F32), axis=1, keepdims=True)

        gate_sum = lax.fori_loop(0, 3, hidden_part, jnp.zeros((320, 1), F32))

        def slot_cols(n, carry):
            cols = pl.ds(pl.multiple_of(n * 256, 256), 256)
            slb[span, cols] = (
                dot_nt(gub[span, 0:768], wg[cols, :]) + dot_nt(gub[span, 768:1536], wu[cols, :])
            ).astype(BF16)
            return carry

        lax.fori_loop(0, 8, slot_cols, 0)

        def pack_back(block, carry):
            pack_block(block, perm_ref[...], slb, send_a)
            return carry

        lax.fori_loop(half * 4, half * 4 + 4, pack_back, 0)
        lane_h = lax.broadcasted_iota(jnp.int32, (HALF, 128), 1)
        tile = jnp.zeros((HALF, 128), F32)
        for r in range(CAP):
            tile = jnp.where(lane_h == r, gate_sum[r * 64 : r * 64 + 64], tile)
        send_a[pl.ds(pl.multiple_of(half * HALF, HALF), HALF), CAP] = jnp.broadcast_to(
            tile[:, None, :], (HALF, 16, 128)
        ).astype(BF16)
        send_group(group, send_a, back, ret_sem.at[0], ret_sem.at[1 + group])

        if group == 0:
            back[pl.ds(me, 1)] = send_a[pl.ds(me, 1)]

    def grad_in(n, carry):
        rows = pl.ds(pl.multiple_of(n * 256, 256), 256)
        out_a[rows, :] = dot_tn(xb[:, rows], gub[:, 0:768]).astype(BF16)
        out_b[rows, :] = dot_tn(xb[:, rows], gub[:, 768:1536]).astype(BF16)
        return carry

    lax.fori_loop(0, 8, grad_in, 0)
    def grad_out(n, carry):
        cols = pl.ds(pl.multiple_of(n * 512, 512), 512)
        out_d[:, cols] = dot_tn(hb[...], yb[:, cols]).astype(BF16)
        return carry

    lax.fori_loop(0, 4, grad_out, 0)

    wait_all(rs1, rs_sem.at[0], 24)
    wait_all(rs2, rs_sem.at[2], 7)
    wait_all(rs2, rs_sem.at[3], 7)
    total = mid[at_m * 2 + zh].astype(F32)
    for s in range(7):
        total = total + rs2[s].astype(F32)
    for h in range(2):
        dk_ref[h * HALF : (h + 1) * HALF, :] = total[h, :, 0:128].astype(BF16)
        dv_ref[h * HALF : (h + 1) * HALF, :] = total[h, :, 128:256].astype(BF16)

    wait_all(send_b, b_sem.at[0], DEVS - 1)
    wait_all(send_a, ret_sem.at[0], DEVS - 1)
    near_spot = lax.broadcasted_iota(jnp.int32, (HALF, HALF), 0)
    gate_rows = [jnp.zeros((1, HALF), F32)] * 8
    for group in range(2):
        half = lax.rem(core + group, 2)
        wait_all(back, ret_sem.at[1 + group], 63 + group)
        unpack(back, slb, half * 4, half * 4 + 4)
        slot_gates = back[pl.ds(half * HALF, HALF), CAP].astype(F32)[:, 0, :]
        acc = jnp.zeros((HALF, HALF), F32)
        for r in range(CAP):
            first = pl.multiple_of(half * 320 + r * 64, 64)
            acc = acc + table[pl.ds(first, 64), :].astype(F32) * slot_gates[:, r : r + 1]
        owner = (near_spot // 2) * 4 + half * 2 + lax.rem(near_spot, 2)
        for j in range(8):
            named_here = owner == ids_ref[j : j + 1, :]
            gate_rows[j] = gate_rows[j] + jnp.sum(
                jnp.where(named_here, acc, 0.0), axis=0, keepdims=True
            )
    for j in range(8):
        dgates_ref[j : j + 1, :] = (gate_rows[j] / gates[j : j + 1, :]).astype(BF16)

    def combine(n, carry):
        cols = pl.ds(pl.multiple_of(n * 512, 512), 512)
        drows_ref[:, cols] = dot_tn(table[...], slb[:, cols]).astype(BF16)
        return carry

    lax.fori_loop(0, 4, combine, 0)


def hand_over(*refs):
    copies = [pltpu.make_async_copy(refs[i], refs[8 + i], refs[16].at[i]) for i in range(8)]
    for copy in reversed(copies):
        copy.start()
    for copy in copies:
        copy.wait()


def shards(
    query_rows,
    key_rows,
    value_rows,
    attn_out,
    attn_grad,
    log_total,
    stretch_order,
    moe_rows,
    moe_grad,
    expert_ids,
    gate_prob,
    gate_weight,
    up_weight,
    down_weight,
):
    tok, heads, size = query_rows.shape
    flat = tok * heads
    rows_here, width = moe_rows.shape
    hidden = gate_weight.shape[2]
    vmem = pl.BlockSpec(memory_space=pltpu.VMEM)
    smem = pl.BlockSpec(memory_space=pltpu.SMEM)
    hbm = pl.BlockSpec(memory_space=pl.ANY)
    chunk = (DEVS, CAP, TILES, 128)
    chunk_and_gates = (DEVS, CAP + 1, TILES, 128)
    slots = DEVS * CAP
    shapes = (
        jax.ShapeDtypeStruct((flat, size), BF16),
        jax.ShapeDtypeStruct((tok, size), BF16),
        jax.ShapeDtypeStruct((tok, size), BF16),
        jax.ShapeDtypeStruct((rows_here, width), BF16),
        jax.ShapeDtypeStruct((8, rows_here), BF16),
        jax.ShapeDtypeStruct((width, hidden), BF16),
        jax.ShapeDtypeStruct((width, hidden), BF16),
        jax.ShapeDtypeStruct((hidden, width), BF16),
    )
    results = pl.pallas_call(
        layer_kernel,
        out_shape=tuple(pltpu.VMEM(shape.shape, BF16) for shape in shapes),
        in_specs=[vmem] * 6 + [smem] + [vmem] * 4 + [hbm] * 3,
        out_specs=(vmem,) * 8,
        scratch_shapes=[
            pltpu.VMEM((2, HALF, 256), BF16),
            pltpu.VMEM((CHIPS, 2, HALF, 256), BF16),
            pltpu.VMEM((CHIPS, 2, HALF, 256), BF16),
            pltpu.VMEM((24, 2, HALF, 256), BF16),
            pltpu.VMEM((8, 2, HALF, 256), BF16),
            pltpu.VMEM((7, 2, HALF, 256), BF16),
            pltpu.VMEM((slots, HALF), BF16),
            pltpu.VMEM((slots, HALF), BF16),
            pltpu.VMEM((2, flat, size), BF16),
            pltpu.VMEM((2, flat, size), BF16),
            pltpu.VMEM((2, 8, flat), F32),
            pltpu.VMEM((2, size, flat), F32),
            pltpu.VMEM((size, flat), F32),
            pltpu.VMEM((256, 256), BF16),
            pltpu.VMEM(chunk_and_gates, BF16),
            pltpu.VMEM(chunk, BF16),
            pltpu.VMEM(chunk, BF16),
            pltpu.VMEM(chunk, BF16),
            pltpu.VMEM(chunk_and_gates, BF16),
            pltpu.VMEM((slots, width), BF16),
            pltpu.VMEM((slots, width), BF16),
            pltpu.VMEM((slots, width), BF16),
            pltpu.VMEM((width, hidden), BF16),
            pltpu.VMEM((width, hidden), BF16),
            pltpu.VMEM((hidden, width), BF16),
            pltpu.VMEM((slots, hidden), F32),
            pltpu.VMEM((slots, hidden), F32),
            pltpu.VMEM((slots, 2 * hidden), BF16),
            pltpu.VMEM((slots, hidden), BF16),
            pltpu.SemaphoreType.DMA((3,)),
            pltpu.SemaphoreType.DMA((4,)),
            pltpu.SemaphoreType.DMA((6,)),
            pltpu.SemaphoreType.DMA((2,)),
            pltpu.SemaphoreType.DMA((3,)),
            pltpu.SemaphoreType.DMA((4,)),
            pltpu.SemaphoreType.DMA((2,)),
            pltpu.SemaphoreType.DMA((3,)),
        ],
        compiler_params=pltpu.CompilerParams(
            collective_id=0, has_side_effects=True, vmem_limit_bytes=52 * 1024 * 1024
        ),
    )(
        query_rows.reshape(flat, size),
        key_rows.reshape(tok, size),
        value_rows.reshape(tok, size),
        attn_out.reshape(flat, size),
        attn_grad.reshape(flat, size),
        log_total.T,
        stretch_order,
        moe_rows,
        moe_grad,
        expert_ids.T,
        gate_prob.T,
        gate_weight[0],
        up_weight[0],
        down_weight[0],
    )
    results = pl.pallas_call(
        hand_over,
        out_shape=shapes,
        in_specs=[hbm] * 8,
        out_specs=(hbm,) * 8,
        scratch_shapes=[pltpu.SemaphoreType.DMA((8,))],
        compiler_params=pltpu.CompilerParams(vmem_limit_bytes=16 * 1024 * 1024),
    )(*results)
    d_query, d_key, d_value, d_rows, d_gates, grad_gate, grad_up, grad_down = results
    return (
        d_query.reshape(tok, heads, size),
        d_key.reshape(tok, 1, size),
        d_value.reshape(tok, 1, size),
        d_rows,
        d_gates.T,
        grad_gate[None],
        grad_up[None],
        grad_down[None],
    )


def solution(mesh):
    both = ("ctx", "kv")
    heads = P("ctx", "kv", None)
    tokens = P(both, None)
    experts = P(both, None, None)
    return jax.shard_map(
        shards,
        mesh=mesh,
        in_specs=(heads,) * 5
        + (P("ctx", "kv"), P())
        + (tokens,) * 4
        + (experts,) * 3,
        out_specs=(heads,) * 3 + (tokens,) * 2 + (experts,) * 3,
        check_vma=False,
    )
```
